256 devices in a mesh: space: 32 (over y, x, core), frame: 8 (over z).
Axes of the slice: x: 4, y: 4, z: 8, core: 2. Of those that a mesh axis runs over, the one named last changes fastest.
Arguments:
- features: bfloat16 [8, 128, 8, 8, 512], P('frame', 'space'), may hold values from -6 to 6
- occupancy: int32 [8, 128, 512], P('frame', 'space'), may hold values 0 or 1
- w_spatial: bfloat16 [2, 27, 64, 64], replicated, may hold values from -0.21875 to 0.21875
- b_spatial: float32 [2, 64], replicated, may hold values from -3 to 3
- w_temporal: bfloat16 [3, 64, 64], replicated, may hold values from -0.75 to 0.75
- face_send: int32 [8, 64], P('frame', 'space'), may hold values from -1 to 19, as said below
- face_source: int32 [8, 128, 6], P('frame', 'space'), may hold values from -1 to 25, as said below
- send_ahead: int32 [8, 96], P('frame', 'space'), may hold values from 0 to 3, as said below
- from_prior: int32 [8, 128], P('frame', 'space'), may hold values from -1 to 2, as said below
- send_back: int32 [8, 96], P('frame', 'space'), may hold values from 0 to 3, as said below
- from_later: int32 [8, 128], P('frame', 'space'), may hold values from -1 to 2, as said below
Outputs:
- section_out: bfloat16 [8, 128, 8, 8, 512], P('frame', 'space')
The draws below stay inside these ranges and needn't reach their ends.
Inputs may be any that keep to these rules, and one draw needn't show every extreme that they name: `face_send`: entries 0 to 0 of a device's row are the faces it sends to the device one lower in space, as brick * 6 + 0 of 1 distinct own bricks; entries 1 to 1 those it sends to the device one higher, as brick * 6 + 1 of 1 distinct own bricks; all -1 toward a side where the axis ends. `face_source`: entry (b, f) names an entry of the device's table: k < 1 a face from the device below (only for f = 0), 1 + k one from the device above (only for f = 1), 2 + 6 j + g face g of brick j of the same device, the opposite of f; or -1. Every received face is named exactly once; local pairs are mutual. `send_ahead`: each device's 3 entries are distinct bricks of that device. `from_prior`: -1 for every brick of frame 0; in other frames exactly 3 bricks of each device name a slot, each slot once. `send_back`: each device's 3 entries are distinct bricks of that device. `from_later`: -1 for every brick of the last frame; in other frames exactly 3 bricks of each device name a slot, each slot once.
All inputs are finite; a program needn't handle non-finite values. No bound on the sum of `occupancy` on one device may be relied on, other than what follows from the above.
Results may differ from the reference program's by a relative error of at most 0.0049.
Values may be sent and summed in bfloat16 or wider, within the bound.
A program may use at most 64 MiB of HBM per device.

```python
import jax
import jax.numpy as jnp
from jax import lax

CH = 64
EDGE = 8
LAYERS = 2
BR = 4
SLABS = 1
MATCH = 3
FRAMES = 8
BRICKS = 128
N_SPACE = 32


def last_first(sub_key):
    order = jax.random.permutation(sub_key, BR).astype(jnp.int32)
    where_last = jnp.argmax(order == BR - 1).astype(jnp.int32)
    order = order.at[where_last].set(order[0])
    return order.at[0].set(BR - 1)


def rim_tables(key):
    base_key = jax.random.fold_in(key, 31)

    def one_device(own_id, orders):
        down_bricks = orders[0, :SLABS].astype(jnp.int32)
        up_bricks = orders[1, :SLABS].astype(jnp.int32)
        slot_ids = jnp.arange(SLABS, dtype=jnp.int32)
        local_base = 2 * SLABS
        naming = jnp.full((BR * 6,), -1, jnp.int32)
        naming = naming.at[jnp.where(own_id > 0, down_bricks * 6, BR * 6)].set(slot_ids, mode='drop')
        naming = naming.at[jnp.where(own_id < N_SPACE - 1, up_bricks * 6 + 1, BR * 6)].set(SLABS + slot_ids, mode='drop')
        pair_count = BR // 4
        for order_row, low_face in ((2, 2), (3, 4)):
            chosen = orders[order_row].astype(jnp.int32)
            first = chosen[0:2 * pair_count:2]
            second = chosen[1:2 * pair_count:2]
            naming = naming.at[second * 6 + low_face].set(local_base + first * 6 + low_face + 1)
            naming = naming.at[first * 6 + low_face + 1].set(local_base + second * 6 + low_face)
        send_low = jnp.where(own_id > 0, down_bricks * 6, -1)
        send_high = jnp.where(own_id < N_SPACE - 1, up_bricks * 6 + 1, -1)
        return (jnp.concatenate([send_low, send_high]), naming.reshape(BR, 6))

    def one_frame(frame_key):
        orders = jax.vmap(last_first)(jax.random.split(frame_key, N_SPACE * 4)).reshape(N_SPACE, 4, BR)
        return jax.vmap(one_device)(jnp.arange(N_SPACE, dtype=jnp.int32), orders)
    sending, naming = jax.vmap(one_frame)(jax.random.split(base_key, FRAMES))
    return (sending.reshape(FRAMES, N_SPACE * 2 * SLABS).astype(jnp.int32), naming.reshape(FRAMES, N_SPACE * BR, 6).astype(jnp.int32))


def frame_links(key, salt_value):
    base_key = jax.random.fold_in(key, salt_value)
    shuffles = jax.vmap(last_first)(jax.random.split(base_key, FRAMES * N_SPACE * 2)).reshape(FRAMES, N_SPACE, 2, BR)
    senders = shuffles[:, :, 0, :MATCH].astype(jnp.int32)
    takers = shuffles[:, :, 1, :MATCH]
    matches = (takers[:, :, :, None] == jnp.arange(BR)[None, None, None, :]).astype(jnp.int32)
    slot_ids = jnp.sum(matches * (jnp.arange(MATCH, dtype=jnp.int32) + 1)[None, None, :, None], axis=2) - 1
    return (senders, slot_ids.astype(jnp.int32))


def draw_face_send(key, part):
    return rim_tables(key)[0]


def draw_face_source(key, part):
    return rim_tables(key)[1]


def draw_send_ahead(key, part):
    senders, slot_ids = frame_links(key, 11)
    return senders.reshape(FRAMES, N_SPACE * MATCH)


def draw_from_prior(key, part):
    senders, slot_ids = frame_links(key, 11)
    first = (jnp.arange(FRAMES) == 0)[:, None, None]
    return jnp.where(first, -1, slot_ids).reshape(FRAMES, N_SPACE * BR).astype(jnp.int32)


def draw_send_back(key, part):
    senders, slot_ids = frame_links(key, 12)
    return senders.reshape(FRAMES, N_SPACE * MATCH)


def draw_from_later(key, part):
    senders, slot_ids = frame_links(key, 12)
    final = (jnp.arange(FRAMES) == FRAMES - 1)[:, None, None]
    return jnp.where(final, -1, slot_ids).reshape(FRAMES, N_SPACE * BR).astype(jnp.int32)


def with_ends(drawn, rng, low, high):
    dims = drawn.shape
    index_at = [jax.random.randint(jax.random.fold_in(rng, axis), (), 0, dims[axis]) for axis in range(len(dims))]
    drawn = drawn.at[tuple(index_at)].set(low)
    longest = dims.index(max(dims))
    index_at[longest] = (index_at[longest] + 1) % dims[longest]
    return drawn.at[tuple(index_at)].set(high)


def levels(rng, extent, cuts, smallest, top_value):
    factor_of = 1.0
    for position, parts in cuts:
        steps = jax.random.uniform(jax.random.fold_in(jax.random.fold_in(rng, 6), position), (parts,), jnp.float32, smallest / len(cuts), top_value / len(cuts))
        factor_of = factor_of * jnp.repeat(jnp.exp(steps), extent[position] // parts).reshape((-1,) + (1,) * (len(extent) - 1 - position))
    return factor_of


def normal_values(key, extent, deviation, bound, cuts=(), kind=jnp.bfloat16):
    entries = jax.random.normal(key, extent, jnp.float32) * deviation
    if len(cuts) > 0:
        entries = levels(key, extent, cuts, -0.22, 0.18) * entries
    return jnp.clip(entries, min=-bound, max=bound).astype(kind)


def setup_inputs(seed: int = 0) -> dict:
    streams_of = jax.random.split(jax.random.key(seed), 12)
    features = normal_values(streams_of[0], (FRAMES, BRICKS, EDGE, EDGE, EDGE * CH), 1.0, 6.0, ((0, 8), (1, 32)))
    occupancy = with_ends((jax.random.randint(streams_of[1], (FRAMES, BRICKS, EDGE * EDGE * EDGE), 0, 4) < 3).astype(jnp.int32), jax.random.fold_in(streams_of[1], 1), 0, 1)
    w_spatial = normal_values(streams_of[2], (LAYERS, 27, CH, CH), (12 * CH) ** -0.5, 0.21875)
    b_spatial = normal_values(streams_of[3], (LAYERS, CH), 0.5, 3.0, (), jnp.float32)
    w_temporal = normal_values(streams_of[4], (3, CH, CH), CH ** -0.5, 0.75)
    face_send = draw_face_send(jax.random.fold_in(streams_of[11], 71), 0)
    face_source = draw_face_source(jax.random.fold_in(streams_of[11], 71), 0)
    send_ahead = draw_send_ahead(jax.random.fold_in(streams_of[11], 71), 0)
    from_prior = draw_from_prior(jax.random.fold_in(streams_of[11], 71), 0)
    send_back = draw_send_back(jax.random.fold_in(streams_of[11], 71), 0)
    from_later = draw_from_later(jax.random.fold_in(streams_of[11], 71), 0)
    return {"features": features, "occupancy": occupancy, "w_spatial": w_spatial, "b_spatial": b_spatial, "w_temporal": w_temporal, "face_send": face_send, "face_source": face_source, "send_ahead": send_ahead, "from_prior": from_prior, "send_back": send_back, "from_later": from_later}


def voxel_mask(occupied, edge_len, channels):
    bricks = occupied.shape[0]
    shaped = occupied.astype(jnp.float32).reshape(bricks, edge_len, edge_len, edge_len, 1)
    return jnp.broadcast_to(shaped, (bricks, edge_len, edge_len, edge_len, channels)).reshape(bricks, edge_len, edge_len, edge_len * channels)


def face_layers(field_data, edge_len, channels):
    bricks = field_data.shape[0]
    volume = field_data.reshape(bricks, edge_len, edge_len, edge_len, channels)
    planes = [volume[:, :, :, 0], volume[:, :, :, edge_len - 1], volume[:, :, 0], volume[:, :, edge_len - 1], volume[:, 0], volume[:, edge_len - 1]]
    stacked = jnp.stack([single.reshape(bricks, edge_len, edge_len * channels) for single in planes], axis=1)
    return stacked.reshape(bricks * 6, edge_len, edge_len * channels)


def padded_block(field_data, rim_faces, edge_len, channels):
    bricks = field_data.shape[0]
    wide_cols = (edge_len + 2) * channels
    inner = slice(1, edge_len + 1)
    middle = slice(channels, (edge_len + 1) * channels)
    padded = jnp.zeros((bricks, edge_len + 2, edge_len + 2, wide_cols), jnp.bfloat16)
    padded = padded.at[:, inner, inner, middle].set(field_data)
    padded = padded.at[:, inner, inner, 0:channels].set(rim_faces[:, 0].reshape(bricks, edge_len, edge_len, channels))
    padded = padded.at[:, inner, inner, (edge_len + 1) * channels:wide_cols].set(rim_faces[:, 1].reshape(bricks, edge_len, edge_len, channels))
    padded = padded.at[:, inner, 0, middle].set(rim_faces[:, 2])
    padded = padded.at[:, inner, edge_len + 1, middle].set(rim_faces[:, 3])
    padded = padded.at[:, 0, inner, middle].set(rim_faces[:, 4])
    padded = padded.at[:, edge_len + 1, inner, middle].set(rim_faces[:, 5])
    return padded


def conv_exact(padded, weights, bias_row, keep_mask, edge_len, channels, group_size):
    bricks = padded.shape[0]

    def one_group(pieces):
        piece_block, piece_mask = pieces
        shifted = []
        for depth_off in range(3):
            for row_off in range(3):
                for col_off in range(3):
                    shifted.append(piece_block[:, depth_off:depth_off + edge_len, row_off:row_off + edge_len, col_off * channels:col_off * channels + edge_len * channels])
        columns = jnp.stack(shifted, axis=1).reshape(group_size, 27, edge_len, edge_len, edge_len, channels)
        summed = jnp.einsum("btzyxc,tcd->bzyxd", columns.astype(jnp.float32), weights.astype(jnp.float32))
        summed = summed.reshape(group_size, edge_len, edge_len, edge_len * channels) + jnp.tile(bias_row, edge_len)
        return (jnp.maximum(summed, 0.0) * piece_mask).astype(jnp.bfloat16)

    grouped = lax.map(one_group, (padded.reshape((bricks // group_size, group_size) + padded.shape[1:]), keep_mask.reshape((bricks // group_size, group_size) + keep_mask.shape[1:])))
    return grouped.reshape(bricks, edge_len, edge_len, edge_len * channels)


def reference(features, occupancy, w_spatial, b_spatial, w_temporal, face_send, face_source, send_ahead, from_prior, send_back, from_later):
    frames = features.shape[0]
    all_bricks = features.shape[1]
    edge_len = features.shape[2]
    channels = w_spatial.shape[-1]
    peers = N_SPACE
    per_dev = all_bricks // peers
    slab_count = face_send.shape[1] // (2 * peers)

    def pick_rows(table, names):
        return jnp.where((names >= 0)[:, None, None], table[jnp.clip(names, 0)], 0)

    def pick_rims(table, names):
        return jnp.where((names >= 0)[:, :, None, None], table[jnp.clip(names, 0)], 0)

    def spatial(packed):
        frame_feats, frame_occ, send_plan, slot_names = packed
        keep_mask = voxel_mask(frame_occ, edge_len, channels)
        inputs = (frame_feats.astype(jnp.float32) * keep_mask).astype(jnp.bfloat16)
        hidden = inputs
        plan_rows = send_plan.reshape(peers, 2 * slab_count)
        local_src = slot_names.reshape(peers, per_dev, 6)
        for layer_index in range(LAYERS):
            face_dev = face_layers(hidden, edge_len, channels).reshape(peers, per_dev * 6, edge_len, edge_len * channels)
            outbound = jax.vmap(pick_rows)(face_dev, plan_rows)
            empty = jnp.zeros_like(outbound[:1, :slab_count])
            from_lower = jnp.concatenate([empty, outbound[:-1, slab_count:]], axis=0)
            from_upper = jnp.concatenate([outbound[1:, :slab_count], empty], axis=0)
            table = jnp.concatenate([from_lower, from_upper, face_dev], axis=1)
            rim_faces = jax.vmap(pick_rims)(table, local_src).reshape(all_bricks, 6, edge_len, edge_len * channels)
            padded = padded_block(hidden, rim_faces, edge_len, channels)
            hidden = conv_exact(padded, w_spatial[layer_index], b_spatial[layer_index], keep_mask, edge_len, channels, 16)
        return inputs, hidden

    inputs_all, hidden_all = lax.map(spatial, (features, occupancy, face_send, face_source))
    device_base = (jnp.arange(peers, dtype=jnp.int32) * per_dev)[:, None]

    def temporal(frame_id):
        hidden = hidden_all[frame_id]
        before_id = jnp.maximum(frame_id - 1, 0)
        after_id = jnp.minimum(frame_id + 1, frames - 1)
        ahead_rows = device_base + send_ahead[before_id].reshape(peers, MATCH)
        prior_slots = from_prior[frame_id].reshape(peers, per_dev)
        chosen = jnp.take_along_axis(ahead_rows, jnp.clip(prior_slots, 0), axis=1).reshape(all_bricks)
        usable = (prior_slots.reshape(all_bricks) >= 0) & (frame_id > 0)
        from_before = jnp.where(usable[:, None, None, None], hidden_all[before_id][chosen], 0)
        back_rows = device_base + send_back[after_id].reshape(peers, MATCH)
        later_slots = from_later[frame_id].reshape(peers, per_dev)
        chosen_after = jnp.take_along_axis(back_rows, jnp.clip(later_slots, 0), axis=1).reshape(all_bricks)
        usable_after = (later_slots.reshape(all_bricks) >= 0) & (frame_id < frames - 1)
        from_after = jnp.where(usable_after[:, None, None, None], hidden_all[after_id][chosen_after], 0)
        temporal_sum = jnp.dot(from_before.reshape(-1, channels), w_temporal[0], preferred_element_type=jnp.float32)
        temporal_sum = temporal_sum + jnp.dot(hidden.reshape(-1, channels), w_temporal[1], preferred_element_type=jnp.float32)
        temporal_sum = temporal_sum + jnp.dot(from_after.reshape(-1, channels), w_temporal[2], preferred_element_type=jnp.float32)
        keep_mask = voxel_mask(occupancy[frame_id], edge_len, channels)
        total_sum = inputs_all[frame_id].astype(jnp.float32) + temporal_sum.reshape(all_bricks, edge_len, edge_len, edge_len * channels)
        return (keep_mask * total_sum).astype(jnp.bfloat16)

    return lax.map(temporal, jnp.arange(frames, dtype=jnp.int32))
```

```python
import jax
import jax.numpy as jnp
from jax import lax
from jax.experimental import pallas as pl
from jax.experimental.pallas import tpu as pltpu
from jax.sharding import PartitionSpec as P

MESH = pl.DeviceIdType.MESH
F32 = jnp.float32
BF16 = jnp.bfloat16
PAIRS = (1, 2, 0, 3)
INNER, OUTER = slice(0, 16), slice(16, 32)


def below(x, edge, row):
    return pltpu.roll(jnp.where(row == 7, edge, x), 1, axis=x.ndim - 2)


def above(x, edge, row):
    return pltpu.roll(jnp.where(row == 0, edge, x), 7, axis=x.ndim - 2)


def three(x, low, high, row):
    return below(x, low, row), x, above(x, high, row)


def pair(a, b):
    return jnp.concatenate([a, b], axis=-2).astype(BF16)


def put_layers(S, dy, at, rows, lanes, x):
    x = x.reshape((4, 2) + x.shape[1:])
    S[1, dy, at, 0:4, rows, lanes] = x[:, 0]
    S[0, dy, at, 1:5, rows, lanes] = x[:, 1]


def left_side(S, rows):
    pieces = []
    for zz in range(4):
        for dy in range(3):
            x = S[zz % 2, dy, :, zz // 2 : zz // 2 + 4, rows, :]
            pieces.append(x.reshape(-1, 256))
    return jnp.concatenate(pieces, axis=1)


def kernel(
    feats, occ, wsp, bsp, wtm, fsend, fsrc, sahead, fprior, sback, flater, out,
    fin, occv, wv, bv, wtv, M, H0, H1, ACC, S1, S2, SV, W, WT, VH, CR, msg, rmsg,
    sE, rE, sL, rL, H2, BASE, lsem, msend, mrecv, esend, erecv, lsend, lrecv,
):
    s, f = lax.axis_index("space"), lax.axis_index("frame")
    n_s, n_f = lax.axis_size("space"), lax.axis_size("frame")
    lo, hi, be, af = s > 0, s < n_s - 1, f > 0, f < n_f - 1

    loads = [
        pltpu.make_async_copy(src, dst, lsem.at[i])
        for i, (src, dst) in enumerate(
            ((occ.at[0], occv), (feats.at[0], fin), (wsp, wv), (bsp, bv), (wtm, wtv))
        )
    ]
    for c in loads:
        c.start()

    barrier = pltpu.get_barrier_semaphore()
    for there, to in (
        (lo, {"space": s - 1}),
        (hi, {"space": s + 1}),
        (be, {"frame": f - 1}),
        (af, {"frame": f + 1}),
    ):

        @pl.when(there)
        def _(to=to):
            pl.semaphore_signal(barrier, 1, device_id=to, device_id_type=MESH)

    lane = lax.broadcasted_iota(jnp.int32, (1, 1, 128), 2)
    left = lane < 64
    row = lax.broadcasted_iota(jnp.int32, (1, 8, 128), 1)
    row2 = lax.broadcasted_iota(jnp.int32, (8, 128), 0)

    loads[0].wait()
    voxel = lax.broadcasted_iota(jnp.int32, (64, 512), 1)
    mine = (voxel >> 3) == lax.broadcasted_iota(jnp.int32, (64, 512), 0)
    o = occv[...].astype(F32)
    spread = jnp.concatenate(
        [jnp.where(mine, o[b : b + 1, :], 0.0).astype(BF16) for b in range(4)], axis=0
    )
    r = lax.broadcasted_iota(jnp.int32, (16, 512), 0) & 7
    c = lax.broadcasted_iota(jnp.int32, (16, 512), 1) >> 6
    widen = jnp.where(r == c, 1.0, 0.0).astype(BF16)
    widen = jnp.concatenate([widen] * 32, axis=0)
    m = jnp.dot(spread, widen, preferred_element_type=F32)
    loads[1].wait()
    for g in range(4):
        mg = m[:, g * 128 : (g + 1) * 128].reshape(4, 4, 2, 8, 128)
        M[:, :, :, g] = mg
        x = fin[:, :, :, g * 128 : (g + 1) * 128].astype(F32)
        H0[:, :, :, g] = x.reshape(4, 4, 2, 8, 128) * mg

    def tile(H, b, g):
        return H[b, :, :, g].reshape(8, 8, 128)

    def rim(b, face):
        e = fsrc[0, b, face]
        return e >= 2, jnp.maximum(e - 2, 0) // 6

    def rim_tile(H, b, face, g):
        has, j = rim(b, face)
        return jnp.where(has, tile(H, j, g), 0.0)

    def rim_layer(H, b, face, g):
        has, j = rim(b, face)
        z = 7 if face == 4 else 0
        return jnp.where(has, H[j, z // 2, z % 2, g], 0.0)

    down = jnp.maximum(fsend[0, 0], 0) // 6
    up = jnp.maximum(fsend[0, 1], 0) // 6

    def rows16(x):
        return x.reshape(-1, 128).astype(BF16).reshape(-1, 16, 128)

    def parcel(k, b, g, face, other):
        beyond = rim_tile(H0, b, face, other)
        mask = tile(M, b, g)
        asked = jnp.where(fsrc[0, b, face] == face, 1.0, 0.0)
        mixed = jnp.where(left, beyond, mask) if k == 0 else jnp.where(left, mask, beyond)
        edges = jnp.where(row == 0, rim_tile(H0, b, 3, g), asked)
        edges = jnp.where(row == 7, rim_tile(H0, b, 2, g), edges)
        msg[k, 0:4] = rows16(tile(H0, b, g))
        msg[k, 4:8] = rows16(mixed)
        msg[k, 8:12] = rows16(edges)
        msg[k, 12] = pair(rim_layer(H0, b, 4, g), rim_layer(H0, b, 5, g))

    parcel(0, up, 3, 1, 0)
    parcel(1, down, 0, 0, 3)

    for k, ends in ((0, s == 0), (1, s == n_s - 1)):

        @pl.when(ends)
        def _(k=k):
            rmsg[k] = jnp.zeros((13, 16, 128), BF16)

    loads[2].wait()
    loads[3].wait()
    nil = jnp.zeros((64, 64), BF16)
    nil_half = jnp.zeros((256, 128), BF16)

    def band(layer):
        for yd in range(3):
            W[layer, yd * 256 : yd * 256 + 256, 128:256] = nil_half
            W[layer, (9 + yd) * 256 : (9 + yd) * 256 + 256, 0:128] = nil_half
        for zd in range(3):
            for yd in range(3):
                w0, w1, w2 = (wv[layer, 9 * zd + 3 * yd + k] for k in range(3))
                block = jnp.concatenate(
                    [
                        jnp.concatenate(ab, axis=1)
                        for ab in ((w1, w0), (w2, w1), (nil, w2), (w0, nil))
                    ],
                    axis=0,
                )
                at = (zd * 3 + yd) * 256
                W[layer, at : at + 256, 0:128] = block
                at = at + 768
                W[layer, at : at + 256, 128:256] = block

    band(0)

    here = lo.astype(jnp.int32) + hi.astype(jnp.int32) + be.astype(jnp.int32) + af.astype(jnp.int32)
    pl.semaphore_wait(barrier, here)

    def remote(src, dst, send, recv, to):
        return pltpu.make_async_remote_copy(
            src_ref=src, dst_ref=dst, send_sem=send, recv_sem=recv, device_id=to, device_id_type=MESH
        )

    upward = remote(msg.at[0], rmsg.at[0], msend.at[0], mrecv.at[0], {"space": s + 1})
    downward = remote(msg.at[1], rmsg.at[1], msend.at[1], mrecv.at[1], {"space": s - 1})

    @pl.when(hi)
    def _():
        upward.start()

    @pl.when(lo)
    def _():
        downward.start()

    band(1)

    def inner_rows(H, S, b):
        t = []
        for g in range(4):
            t.append(three(tile(H, b, g), rim_tile(H, b, 2, g), rim_tile(H, b, 3, g), row))
        for dy in range(3):
            put_layers(S, dy, b, INNER, slice(0, 128), pair(t[1][dy], t[2][dy]))
            e1 = jnp.where(left, t[2][dy], t[0][dy])
            e2 = jnp.where(left, t[3][dy], t[1][dy])
            put_layers(S, dy, b, INNER, slice(128, 256), pair(e1, e2))
        for face, at in ((4, (0, 0)), (5, (1, 4))):
            t = [three(rim_layer(H, b, face, g), 0.0, 0.0, row2) for g in range(4)]
            for dy in range(3):
                S[at[0], dy, b, at[1], INNER, 0:128] = pair(t[1][dy], t[2][dy])
                e1 = jnp.where(left[0], t[2][dy], t[0][dy])
                e2 = jnp.where(left[0], t[3][dy], t[1][dy])
                S[at[0], dy, b, at[1], INNER, 128:256] = pair(e1, e2)

    def outer_rows(H, S, b, xl, xr):
        t = {}
        for g in range(4):
            t[g] = three(tile(H, b, g), rim_tile(H, b, 2, g), rim_tile(H, b, 3, g), row)
        xl = three(xl, 0.0, 0.0, row)
        xr = three(xr, 0.0, 0.0, row)
        for dy in range(3):
            put_layers(S, dy, b, OUTER, slice(0, 128), pair(t[0][dy], t[3][dy]))
            e0 = jnp.where(left, t[1][dy], xl[dy])
            e3 = jnp.where(left, xr[dy], t[2][dy])
            put_layers(S, dy, b, OUTER, slice(128, 256), pair(e0, e3))
        for face, at in ((4, (0, 0)), (5, (1, 4))):
            t = [three(rim_layer(H, b, face, g), 0.0, 0.0, row2) for g in range(4)]
            for dy in range(3):
                S[at[0], dy, b, at[1], OUTER, 0:128] = pair(t[0][dy], t[3][dy])
                e0 = jnp.where(left[0], t[1][dy], 0.0)
                e3 = jnp.where(left[0], 0.0, t[2][dy])
                S[at[0], dy, b, at[1], OUTER, 128:256] = pair(e0, e3)

    @pl.loop(0, 4)
    def _(b):
        inner_rows(H0, S1, b)
        outer_rows(H0, S1, b, rim_tile(H0, b, 0, 3), rim_tile(H0, b, 1, 0))

    bias = [jnp.concatenate([bv[i : i + 1, :]] * 2, axis=1).reshape(1, 1, 1, 128) for i in range(2)]

    acc = jnp.dot(left_side(S1, slice(0, 32)), W[0], preferred_element_type=F32)
    acc = acc.reshape(4, 4, 4, 8, 256)
    for i, g in enumerate(PAIRS):
        for oz in range(2):
            h = acc[:, :, i, :, oz * 128 : (oz + 1) * 128] + bias[0]
            if i >= 2:
                ACC[:, :, oz, i - 2] = h
            H1[:, :, oz, g] = jnp.maximum(h, 0.0) * M[:, :, oz, g]

    @pl.loop(0, 4)
    def _(b):
        inner_rows(H1, S2, b)

    def second(half):
        rows = (INNER, OUTER)[half]
        acc = jnp.dot(left_side(S2, rows), W[1], preferred_element_type=F32)
        acc = acc.reshape(4, 4, 2, 8, 256)
        for i in range(2):
            g = PAIRS[2 * half + i]
            h = [
                jnp.maximum(acc[:, :, i, :, oz * 128 : (oz + 1) * 128] + bias[1], 0.0)
                * M[:, :, oz, g]
                for oz in range(2)
            ]
            H2[half, :, :, :, i * 128 : (i + 1) * 128] = jnp.concatenate(h, axis=2).astype(BF16)

    def exchange(half, sent, got, send, recv):
        for k in range(3):
            sent[0, k] = H2[half, sahead[0, k]]
            sent[1, k] = H2[half, sback[0, k]]
        ahead = remote(sent.at[0], got.at[0], send.at[0], recv.at[0], {"frame": f + 1})
        back = remote(sent.at[1], got.at[1], send.at[1], recv.at[1], {"frame": f - 1})

        @pl.when(af)
        def _():
            ahead.start()

        @pl.when(be)
        def _():
            back.start()

        return ahead, back

    second(0)
    early = exchange(0, sE, rE, esend, erecv)

    loads[4].wait()
    for k in range(3):
        w = wtv[k]
        two = jnp.concatenate(
            [jnp.concatenate([w, nil], axis=1), jnp.concatenate([nil, w], axis=1)], axis=0
        )
        WT[k, 0:128, 0:128] = two
        WT[k, 128:256, 128:256] = two
        WT[k, 0:128, 128:256] = jnp.zeros((128, 128), BF16)
        WT[k, 128:256, 0:128] = jnp.zeros((128, 128), BF16)

    def wide(H, g):
        return H[:, :, :, g].reshape(4, 4, 16, 128)

    def base(half):
        t = jnp.dot(H2[half].reshape(256, 256), WT[1], preferred_element_type=F32)
        t = t.reshape(4, 4, 16, 256)
        for i in range(2):
            g = PAIRS[2 * half + i]
            lanes = slice(i * 128, (i + 1) * 128)
            BASE[half, :, :, :, lanes] = t[:, :, :, lanes] + wide(H0, g)

    base(0)

    for there, copy in ((lo, upward), (hi, downward)):

        @pl.when(there)
        def _(copy=copy):
            copy.wait_recv()

    def parts(k):
        x = rmsg[k].astype(F32)
        return (
            x[0:4].reshape(8, 8, 128),
            x[4:8].reshape(8, 8, 128),
            x[8:12].reshape(8, 8, 128),
            x[12].reshape(2, 8, 128),
        )

    got = [parts(0), parts(1)]
    own = (tile(H0, down, 0), tile(H0, up, 3))
    V = []
    for k in range(2):
        a, b, e, z = got[k]
        beyond = jnp.where(e[:, 3:4, :] > 0.5, own[k], b)
        V.append((three(a, e, e, row), three(beyond, 0.0, 0.0, row), three(z, 0.0, 0.0, row)))
    zero = jnp.zeros((8, 8, 128), F32)
    thin = jnp.zeros((16, 128), BF16)
    for dy in range(3):
        put_layers(SV, dy, 0, INNER, slice(0, 128), pair(V[0][0][dy], V[1][0][dy]))
        put_layers(SV, dy, 0, INNER, slice(128, 256), pair(V[0][1][dy], V[1][1][dy]))
        put_layers(SV, dy, 0, OUTER, slice(0, 128), pair(zero, zero))
        x0 = jnp.where(left, 0.0, three(got[0][0], 0.0, 0.0, row)[dy])
        x1 = jnp.where(left, three(got[1][0], 0.0, 0.0, row)[dy], 0.0)
        put_layers(SV, dy, 0, OUTER, slice(128, 256), pair(x0, x1))
        for z, at in ((0, (0, 0)), (1, (1, 4))):
            SV[at[0], dy, 0, at[1], INNER, 0:128] = pair(V[0][2][dy][z], V[1][2][dy][z])
            SV[at[0], dy, 0, at[1], INNER, 128:256] = thin
            SV[at[0], dy, 0, at[1], OUTER, 0:128] = thin
            SV[at[0], dy, 0, at[1], OUTER, 128:256] = thin

    acc = jnp.dot(left_side(SV, slice(0, 32)), W[0], preferred_element_type=F32)
    acc = acc.reshape(4, 4, 8, 256)
    for k in range(2):
        for oz in range(2):
            lanes = slice(oz * 128, (oz + 1) * 128)
            mask = got[k][1].reshape(4, 2, 8, 128)[:, oz]
            VH[k, :, oz] = jnp.maximum(acc[:, k, :, lanes] + bias[0][0], 0.0) * mask
            CR[k, :, oz] = acc[:, 2 + k, :, lanes]

    @pl.loop(0, 4)
    def _(b):
        for k, g in ((0, 0), (1, 3)):
            h = ACC[b, :, :, k] + jnp.where(fsrc[0, b, k] == k, CR[k], 0.0)
            H1[b, :, :, g] = jnp.maximum(h, 0.0) * M[b, :, :, g]

    @pl.loop(0, 4)
    def _(b):
        x = []
        for k, g in ((0, 3), (1, 0)):
            far = VH[k].reshape(8, 8, 128)
            x.append(jnp.where(fsrc[0, b, k] == k, far, rim_tile(H1, b, k, g)))
        outer_rows(H1, S2, b, x[0], x[1])

    second(1)
    late = exchange(1, sL, rL, lsend, lrecv)
    base(1)

    def finish(half, copies, got):
        ahead, back = copies

        @pl.when(be)
        def _():
            ahead.wait_recv()

        @pl.when(af)
        def _():
            back.wait_recv()

        lhs = []
        for b in range(4):
            p, q = fprior[0, b], flater[0, b]
            x = jnp.where(p >= 0, got[0, jnp.maximum(p, 0)].astype(F32), 0.0).astype(BF16)
            y = jnp.where(q >= 0, got[1, jnp.maximum(q, 0)].astype(F32), 0.0).astype(BF16)
            lhs.append(jnp.concatenate([x.reshape(64, 256), y.reshape(64, 256)], axis=1))
        wt = jnp.concatenate([WT[0], WT[2]], axis=0)
        t = jnp.dot(jnp.concatenate(lhs, axis=0), wt, preferred_element_type=F32)
        t = t.reshape(4, 4, 16, 256)
        for i in range(2):
            g = PAIRS[2 * half + i]
            lanes = slice(i * 128, (i + 1) * 128)
            x = (BASE[half, :, :, :, lanes] + t[:, :, :, lanes]) * wide(M, g)
            out[0, :, :, :, g * 128 : (g + 1) * 128] = x.reshape(4, 8, 8, 128).astype(BF16)

    finish(0, early, rE)
    finish(1, late, rL)

    for there, copies in (
        (hi, (upward,)),
        (lo, (downward,)),
        (af, (early[0], late[0])),
        (be, (early[1], late[1])),
    ):

        @pl.when(there)
        def _(copies=copies):
            for c in copies:
                c.wait_send()


def per_device(*args):
    field = (4, 4, 2, 4, 8, 128)
    hbm = pl.BlockSpec(memory_space=pltpu.HBM)
    smem = pl.BlockSpec(memory_space=pltpu.SMEM)
    left = (2, 3, 4, 5, 32, 256)
    parcels = (2, 3, 4, 16, 256)
    return pl.pallas_call(
        kernel,
        out_shape=pltpu.VMEM((1, 4, 8, 8, 512), BF16),
        in_specs=[hbm] * 5 + [smem] * 6,
        out_specs=pl.BlockSpec(memory_space=pltpu.VMEM),
        scratch_shapes=[
            pltpu.VMEM((4, 8, 8, 512), BF16),
            pltpu.VMEM((4, 512), jnp.int32),
            pltpu.VMEM((2, 27, 64, 64), BF16),
            pltpu.VMEM((2, 64), F32),
            pltpu.VMEM((3, 64, 64), BF16),
            pltpu.VMEM(field, F32),
            pltpu.VMEM(field, F32),
            pltpu.VMEM(field, F32),
            pltpu.VMEM((4, 4, 2, 2, 8, 128), F32),
            pltpu.VMEM(left, BF16),
            pltpu.VMEM(left, BF16),
            pltpu.VMEM((2, 3, 1, 5, 32, 256), BF16),
            pltpu.VMEM((2, 3072, 256), BF16),
            pltpu.VMEM((3, 256, 256), BF16),
            pltpu.VMEM((2, 4, 2, 8, 128), F32),
            pltpu.VMEM((2, 4, 2, 8, 128), F32),
            pltpu.VMEM((2, 13, 16, 128), BF16),
            pltpu.VMEM((2, 13, 16, 128), BF16),
            pltpu.VMEM(parcels, BF16),
            pltpu.VMEM(parcels, BF16),
            pltpu.VMEM(parcels, BF16),
            pltpu.VMEM(parcels, BF16),
            pltpu.VMEM((2, 4, 4, 16, 256), BF16),
            pltpu.VMEM((2, 4, 4, 16, 256), F32),
            pltpu.SemaphoreType.DMA((5,)),
        ]
        + [pltpu.SemaphoreType.DMA((2,))] * 6,
        compiler_params=pltpu.CompilerParams(
            collective_id=0, has_side_effects=True, vmem_limit_bytes=40 << 20
        ),
    )(*args)


def solution(mesh):
    in_specs = (
        P("frame", "space", None, None, None),
        P("frame", "space", None),
        P(),
        P(),
        P(),
        P("frame", "space"),
        P("frame", "space", None),
        P("frame", "space"),
        P("frame", "space"),
        P("frame", "space"),
        P("frame", "space"),
    )
    out_specs = P("frame", "space", None, None, None)
    return jax.shard_map(
        per_device, mesh=mesh, in_specs=in_specs, out_specs=out_specs, check_vma=False
    )
```

```python
import jax
import jax.numpy as jnp
from jax import lax
from jax.experimental import pallas as pl
from jax.experimental.pallas import tpu as pltpu
from jax.sharding import PartitionSpec as P

MESH = pl.DeviceIdType.MESH
F32 = jnp.float32
BF16 = jnp.bfloat16
PAIRS = (1, 2, 0, 3)
INNER, OUTER = slice(0, 16), slice(16, 32)


def below(x, edge, row):
    return pltpu.roll(jnp.where(row == 7, edge, x), 1, axis=x.ndim - 2)


def above(x, edge, row):
    return pltpu.roll(jnp.where(row == 0, edge, x), 7, axis=x.ndim - 2)


def three(x, low, high, row):
    return below(x, low, row), x, above(x, high, row)


def pair(a, b):
    return jnp.concatenate([a, b], axis=-2).astype(BF16)


def put_layers(S, dy, at, rows, lanes, x):
    x = x.reshape((4, 2) + x.shape[1:])
    S[1, dy, at, 0:4, rows, lanes] = x[:, 0]
    S[0, dy, at, 1:5, rows, lanes] = x[:, 1]


def left_side(S, rows):
    pieces = []
    for zz in range(4):
        for dy in range(3):
            x = S[zz % 2, dy, :, zz // 2 : zz // 2 + 4, rows, :]
            pieces.append(x.reshape(-1, 256))
    return jnp.concatenate(pieces, axis=1)


def kernel(
    feats, occ, wsp, bsp, wtm, fsend_h, fsrc_h, sahead_h, fprior_h, sback_h, flater_h, out,
    fsend, fsrc, sahead, fprior, sback, flater, fin, occv, wv, bv, wtv, M, H0, H1, ACC, S1, S2, SV, W, WT, VH, CR, msg, rmsg,
    sE, rE, sL, rL, H2, BASE, lsem, msend, mrecv, esend, erecv, lsend, lrecv,
):
    s, f = lax.axis_index("space"), lax.axis_index("frame")
    n_s, n_f = lax.axis_size("space"), lax.axis_size("frame")
    lo, hi, be, af = s > 0, s < n_s - 1, f > 0, f < n_f - 1

    loads = [
        pltpu.make_async_copy(src, dst, lsem.at[i])
        for i, (src, dst) in enumerate(
            (
                (occ.at[0], occv), (feats.at[0], fin), (wsp, wv), (bsp, bv), (wtm, wtv),
                (fsend_h, fsend), (fsrc_h, fsrc), (sahead_h, sahead), (fprior_h, fprior),
                (sback_h, sback), (flater_h, flater),
            )
        )
    ]
    for c in loads:
        c.start()

    barrier = pltpu.get_barrier_semaphore()
    for there, to in (
        (lo, {"space": s - 1}),
        (hi, {"space": s + 1}),
        (be, {"frame": f - 1}),
        (af, {"frame": f + 1}),
    ):

        @pl.when(there)
        def _(to=to):
            pl.semaphore_signal(barrier, 1, device_id=to, device_id_type=MESH)

    lane = lax.broadcasted_iota(jnp.int32, (1, 1, 128), 2)
    left = lane < 64
    row = lax.broadcasted_iota(jnp.int32, (1, 8, 128), 1)
    row2 = lax.broadcasted_iota(jnp.int32, (8, 128), 0)

    loads[0].wait()
    voxel = lax.broadcasted_iota(jnp.int32, (64, 512), 1)
    mine = (voxel >> 3) == lax.broadcasted_iota(jnp.int32, (64, 512), 0)
    o = occv[...].astype(F32)
    spread = jnp.concatenate(
        [jnp.where(mine, o[b : b + 1, :], 0.0).astype(BF16) for b in range(4)], axis=0
    )
    r = lax.broadcasted_iota(jnp.int32, (16, 512), 0) & 7
    c = lax.broadcasted_iota(jnp.int32, (16, 512), 1) >> 6
    widen = jnp.where(r == c, 1.0, 0.0).astype(BF16)
    widen = jnp.concatenate([widen] * 32, axis=0)
    m = jnp.dot(spread, widen, preferred_element_type=F32)
    loads[1].wait()
    for g in range(4):
        mg = m[:, g * 128 : (g + 1) * 128].reshape(4, 4, 2, 8, 128)
        M[:, :, :, g] = mg
        x = fin[:, :, :, g * 128 : (g + 1) * 128].astype(F32)
        H0[:, :, :, g] = x.reshape(4, 4, 2, 8, 128) * mg

    for copy in loads[5:]:
        copy.wait()

    def tile(H, b, g):
        return H[b, :, :, g].reshape(8, 8, 128)

    def rim(b, face):
        e = fsrc[0, b, face]
        return e >= 2, jnp.maximum(e - 2, 0) // 6

    def rim_tile(H, b, face, g):
        has, j = rim(b, face)
        return jnp.where(has, tile(H, j, g), 0.0)

    def rim_layer(H, b, face, g):
        has, j = rim(b, face)
        z = 7 if face == 4 else 0
        return jnp.where(has, H[j, z // 2, z % 2, g], 0.0)

    down = jnp.maximum(fsend[0, 0], 0) // 6
    up = jnp.maximum(fsend[0, 1], 0) // 6

    def rows16(x):
        return x.reshape(-1, 128).astype(BF16).reshape(-1, 16, 128)

    def parcel(k, b, g, face, other):
        beyond = rim_tile(H0, b, face, other)
        mask = tile(M, b, g)
        asked = jnp.where(fsrc[0, b, face] == face, 1.0, 0.0)
        mixed = jnp.where(left, beyond, mask) if k == 0 else jnp.where(left, mask, beyond)
        edges = jnp.where(row == 0, rim_tile(H0, b, 3, g), asked)
        edges = jnp.where(row == 7, rim_tile(H0, b, 2, g), edges)
        msg[k, 0:4] = rows16(tile(H0, b, g))
        msg[k, 4:8] = rows16(mixed)
        msg[k, 8:12] = rows16(edges)
        msg[k, 12] = pair(rim_layer(H0, b, 4, g), rim_layer(H0, b, 5, g))

    parcel(0, up, 3, 1, 0)
    parcel(1, down, 0, 0, 3)

    for k, ends in ((0, s == 0), (1, s == n_s - 1)):

        @pl.when(ends)
        def _(k=k):
            rmsg[k] = jnp.zeros((13, 16, 128), BF16)

    loads[2].wait()
    loads[3].wait()
    nil = jnp.zeros((64, 64), BF16)
    nil_half = jnp.zeros((256, 128), BF16)

    def band(layer):
        for yd in range(3):
            W[layer, yd * 256 : yd * 256 + 256, 128:256] = nil_half
            W[layer, (9 + yd) * 256 : (9 + yd) * 256 + 256, 0:128] = nil_half
        for zd in range(3):
            for yd in range(3):
                w0, w1, w2 = (wv[layer, 9 * zd + 3 * yd + k] for k in range(3))
                block = jnp.concatenate(
                    [
                        jnp.concatenate(ab, axis=1)
                        for ab in ((w1, w0), (w2, w1), (nil, w2), (w0, nil))
                    ],
                    axis=0,
                )
                at = (zd * 3 + yd) * 256
                W[layer, at : at + 256, 0:128] = block
                at = at + 768
                W[layer, at : at + 256, 128:256] = block

    band(0)

    here = lo.astype(jnp.int32) + hi.astype(jnp.int32) + be.astype(jnp.int32) + af.astype(jnp.int32)
    pl.semaphore_wait(barrier, here)

    def remote(src, dst, send, recv, to):
        return pltpu.make_async_remote_copy(
            src_ref=src, dst_ref=dst, send_sem=send, recv_sem=recv, device_id=to, device_id_type=MESH
        )

    upward = remote(msg.at[0], rmsg.at[0], msend.at[0], mrecv.at[0], {"space": s + 1})
    downward = remote(msg.at[1], rmsg.at[1], msend.at[1], mrecv.at[1], {"space": s - 1})

    @pl.when(hi)
    def _():
        upward.start()

    @pl.when(lo)
    def _():
        downward.start()

    band(1)

    def inner_rows(H, S, b):
        t = []
        for g in range(4):
            t.append(three(tile(H, b, g), rim_tile(H, b, 2, g), rim_tile(H, b, 3, g), row))
        for dy in range(3):
            put_layers(S, dy, b, INNER, slice(0, 128), pair(t[1][dy], t[2][dy]))
            e1 = jnp.where(left, t[2][dy], t[0][dy])
            e2 = jnp.where(left, t[3][dy], t[1][dy])
            put_layers(S, dy, b, INNER, slice(128, 256), pair(e1, e2))
        for face, at in ((4, (0, 0)), (5, (1, 4))):
            t = [three(rim_layer(H, b, face, g), 0.0, 0.0, row2) for g in range(4)]
            for dy in range(3):
                S[at[0], dy, b, at[1], INNER, 0:128] = pair(t[1][dy], t[2][dy])
                e1 = jnp.where(left[0], t[2][dy], t[0][dy])
                e2 = jnp.where(left[0], t[3][dy], t[1][dy])
                S[at[0], dy, b, at[1], INNER, 128:256] = pair(e1, e2)

    def outer_rows(H, S, b, xl, xr):
        t = {}
        for g in range(4):
            t[g] = three(tile(H, b, g), rim_tile(H, b, 2, g), rim_tile(H, b, 3, g), row)
        xl = three(xl, 0.0, 0.0, row)
        xr = three(xr, 0.0, 0.0, row)
        for dy in range(3):
            put_layers(S, dy, b, OUTER, slice(0, 128), pair(t[0][dy], t[3][dy]))
            e0 = jnp.where(left, t[1][dy], xl[dy])
            e3 = jnp.where(left, xr[dy], t[2][dy])
            put_layers(S, dy, b, OUTER, slice(128, 256), pair(e0, e3))
        for face, at in ((4, (0, 0)), (5, (1, 4))):
            t = [three(rim_layer(H, b, face, g), 0.0, 0.0, row2) for g in range(4)]
            for dy in range(3):
                S[at[0], dy, b, at[1], OUTER, 0:128] = pair(t[0][dy], t[3][dy])
                e0 = jnp.where(left[0], t[1][dy], 0.0)
                e3 = jnp.where(left[0], 0.0, t[2][dy])
                S[at[0], dy, b, at[1], OUTER, 128:256] = pair(e0, e3)

    @pl.loop(0, 4)
    def _(b):
        inner_rows(H0, S1, b)
        outer_rows(H0, S1, b, rim_tile(H0, b, 0, 3), rim_tile(H0, b, 1, 0))

    bias = [jnp.concatenate([bv[i : i + 1, :]] * 2, axis=1).reshape(1, 1, 1, 128) for i in range(2)]

    acc = jnp.dot(left_side(S1, slice(0, 32)), W[0], preferred_element_type=F32)
    acc = acc.reshape(4, 4, 4, 8, 256)
    for i, g in enumerate(PAIRS):
        for oz in range(2):
            h = acc[:, :, i, :, oz * 128 : (oz + 1) * 128] + bias[0]
            if i >= 2:
                ACC[:, :, oz, i - 2] = h
            H1[:, :, oz, g] = jnp.maximum(h, 0.0) * M[:, :, oz, g]

    @pl.loop(0, 4)
    def _(b):
        inner_rows(H1, S2, b)

    def second(half):
        rows = (INNER, OUTER)[half]
        acc = jnp.dot(left_side(S2, rows), W[1], preferred_element_type=F32)
        acc = acc.reshape(4, 4, 2, 8, 256)
        for i in range(2):
            g = PAIRS[2 * half + i]
            h = [
                jnp.maximum(acc[:, :, i, :, oz * 128 : (oz + 1) * 128] + bias[1], 0.0)
                * M[:, :, oz, g]
                for oz in range(2)
            ]
            H2[half, :, :, :, i * 128 : (i + 1) * 128] = jnp.concatenate(h, axis=2).astype(BF16)

    def exchange(half, sent, got, send, recv):
        for k in range(3):
            sent[0, k] = H2[half, sahead[0, k]]
            sent[1, k] = H2[half, sback[0, k]]
        ahead = remote(sent.at[0], got.at[0], send.at[0], recv.at[0], {"frame": f + 1})
        back = remote(sent.at[1], got.at[1], send.at[1], recv.at[1], {"frame": f - 1})

        @pl.when(af)
        def _():
            ahead.start()

        @pl.when(be)
        def _():
            back.start()

        return ahead, back

    second(0)
    early = exchange(0, sE, rE, esend, erecv)

    loads[4].wait()
    for k in range(3):
        w = wtv[k]
        two = jnp.concatenate(
            [jnp.concatenate([w, nil], axis=1), jnp.concatenate([nil, w], axis=1)], axis=0
        )
        WT[k, 0:128, 0:128] = two
        WT[k, 128:256, 128:256] = two
        WT[k, 0:128, 128:256] = jnp.zeros((128, 128), BF16)
        WT[k, 128:256, 0:128] = jnp.zeros((128, 128), BF16)

    def wide(H, g):
        return H[:, :, :, g].reshape(4, 4, 16, 128)

    def base(half):
        t = jnp.dot(H2[half].reshape(256, 256), WT[1], preferred_element_type=F32)
        t = t.reshape(4, 4, 16, 256)
        for i in range(2):
            g = PAIRS[2 * half + i]
            lanes = slice(i * 128, (i + 1) * 128)
            BASE[half, :, :, :, lanes] = t[:, :, :, lanes] + wide(H0, g)

    base(0)

    for there, copy in ((lo, upward), (hi, downward)):

        @pl.when(there)
        def _(copy=copy):
            copy.wait_recv()

    def parts(k):
        x = rmsg[k].astype(F32)
        return (
            x[0:4].reshape(8, 8, 128),
            x[4:8].reshape(8, 8, 128),
            x[8:12].reshape(8, 8, 128),
            x[12].reshape(2, 8, 128),
        )

    got = [parts(0), parts(1)]
    own = (tile(H0, down, 0), tile(H0, up, 3))
    V = []
    for k in range(2):
        a, b, e, z = got[k]
        beyond = jnp.where(e[:, 3:4, :] > 0.5, own[k], b)
        V.append((three(a, e, e, row), three(beyond, 0.0, 0.0, row), three(z, 0.0, 0.0, row)))
    zero = jnp.zeros((8, 8, 128), F32)
    thin = jnp.zeros((16, 128), BF16)
    for dy in range(3):
        put_layers(SV, dy, 0, INNER, slice(0, 128), pair(V[0][0][dy], V[1][0][dy]))
        put_layers(SV, dy, 0, INNER, slice(128, 256), pair(V[0][1][dy], V[1][1][dy]))
        put_layers(SV, dy, 0, OUTER, slice(0, 128), pair(zero, zero))
        x0 = jnp.where(left, 0.0, three(got[0][0], 0.0, 0.0, row)[dy])
        x1 = jnp.where(left, three(got[1][0], 0.0, 0.0, row)[dy], 0.0)
        put_layers(SV, dy, 0, OUTER, slice(128, 256), pair(x0, x1))
        for z, at in ((0, (0, 0)), (1, (1, 4))):
            SV[at[0], dy, 0, at[1], INNER, 0:128] = pair(V[0][2][dy][z], V[1][2][dy][z])
            SV[at[0], dy, 0, at[1], INNER, 128:256] = thin
            SV[at[0], dy, 0, at[1], OUTER, 0:128] = thin
            SV[at[0], dy, 0, at[1], OUTER, 128:256] = thin

    acc = jnp.dot(left_side(SV, slice(0, 32)), W[0], preferred_element_type=F32)
    acc = acc.reshape(4, 4, 8, 256)
    for k in range(2):
        for oz in range(2):
            lanes = slice(oz * 128, (oz + 1) * 128)
            mask = got[k][1].reshape(4, 2, 8, 128)[:, oz]
            VH[k, :, oz] = jnp.maximum(acc[:, k, :, lanes] + bias[0][0], 0.0) * mask
            CR[k, :, oz] = acc[:, 2 + k, :, lanes]

    @pl.loop(0, 4)
    def _(b):
        for k, g in ((0, 0), (1, 3)):
            h = ACC[b, :, :, k] + jnp.where(fsrc[0, b, k] == k, CR[k], 0.0)
            H1[b, :, :, g] = jnp.maximum(h, 0.0) * M[b, :, :, g]

    @pl.loop(0, 4)
    def _(b):
        x = []
        for k, g in ((0, 3), (1, 0)):
            far = VH[k].reshape(8, 8, 128)
            x.append(jnp.where(fsrc[0, b, k] == k, far, rim_tile(H1, b, k, g)))
        outer_rows(H1, S2, b, x[0], x[1])

    second(1)
    late = exchange(1, sL, rL, lsend, lrecv)
    base(1)

    def finish(half, copies, got):
        ahead, back = copies

        @pl.when(be)
        def _():
            ahead.wait_recv()

        @pl.when(af)
        def _():
            back.wait_recv()

        lhs = []
        for b in range(4):
            p, q = fprior[0, b], flater[0, b]
            x = jnp.where(p >= 0, got[0, jnp.maximum(p, 0)].astype(F32), 0.0).astype(BF16)
            y = jnp.where(q >= 0, got[1, jnp.maximum(q, 0)].astype(F32), 0.0).astype(BF16)
            lhs.append(jnp.concatenate([x.reshape(64, 256), y.reshape(64, 256)], axis=1))
        wt = jnp.concatenate([WT[0], WT[2]], axis=0)
        t = jnp.dot(jnp.concatenate(lhs, axis=0), wt, preferred_element_type=F32)
        t = t.reshape(4, 4, 16, 256)
        for i in range(2):
            g = PAIRS[2 * half + i]
            lanes = slice(i * 128, (i + 1) * 128)
            x = (BASE[half, :, :, :, lanes] + t[:, :, :, lanes]) * wide(M, g)
            out[0, :, :, :, g * 128 : (g + 1) * 128] = x.reshape(4, 8, 8, 128).astype(BF16)

    finish(0, early, rE)
    finish(1, late, rL)

    for there, copies in (
        (hi, (upward,)),
        (lo, (downward,)),
        (af, (early[0], late[0])),
        (be, (early[1], late[1])),
    ):

        @pl.when(there)
        def _(copies=copies):
            for c in copies:
                c.wait_send()


def per_device(*args):
    field = (4, 4, 2, 4, 8, 128)
    hbm = pl.BlockSpec(memory_space=pltpu.HBM)
    left = (2, 3, 4, 5, 32, 256)
    parcels = (2, 3, 4, 16, 256)
    return pl.pallas_call(
        kernel,
        out_shape=pltpu.VMEM((1, 4, 8, 8, 512), BF16),
        in_specs=[hbm] * 11,
        out_specs=pl.BlockSpec(memory_space=pltpu.VMEM),
        scratch_shapes=[
            pltpu.SMEM((1, 2), jnp.int32),
            pltpu.SMEM((1, 4, 6), jnp.int32),
            pltpu.SMEM((1, 3), jnp.int32),
            pltpu.SMEM((1, 4), jnp.int32),
            pltpu.SMEM((1, 3), jnp.int32),
            pltpu.SMEM((1, 4), jnp.int32),
            pltpu.VMEM((4, 8, 8, 512), BF16),
            pltpu.VMEM((4, 512), jnp.int32),
            pltpu.VMEM((2, 27, 64, 64), BF16),
            pltpu.VMEM((2, 64), F32),
            pltpu.VMEM((3, 64, 64), BF16),
            pltpu.VMEM(field, F32),
            pltpu.VMEM(field, F32),
            pltpu.VMEM(field, F32),
            pltpu.VMEM((4, 4, 2, 2, 8, 128), F32),
            pltpu.VMEM(left, BF16),
            pltpu.VMEM(left, BF16),
            pltpu.VMEM((2, 3, 1, 5, 32, 256), BF16),
            pltpu.VMEM((2, 3072, 256), BF16),
            pltpu.VMEM((3, 256, 256), BF16),
            pltpu.VMEM((2, 4, 2, 8, 128), F32),
            pltpu.VMEM((2, 4, 2, 8, 128), F32),
            pltpu.VMEM((2, 13, 16, 128), BF16),
            pltpu.VMEM((2, 13, 16, 128), BF16),
            pltpu.VMEM(parcels, BF16),
            pltpu.VMEM(parcels, BF16),
            pltpu.VMEM(parcels, BF16),
            pltpu.VMEM(parcels, BF16),
            pltpu.VMEM((2, 4, 4, 16, 256), BF16),
            pltpu.VMEM((2, 4, 4, 16, 256), F32),
            pltpu.SemaphoreType.DMA((11,)),
        ]
        + [pltpu.SemaphoreType.DMA((2,))] * 6,
        compiler_params=pltpu.CompilerParams(
            collective_id=0, has_side_effects=True, vmem_limit_bytes=56 << 20
        ),
    )(*args)


def solution(mesh):
    in_specs = (
        P("frame", "space", None, None, None),
        P("frame", "space", None),
        P(),
        P(),
        P(),
        P("frame", "space"),
        P("frame", "space", None),
        P("frame", "space"),
        P("frame", "space"),
        P("frame", "space"),
        P("frame", "space"),
    )
    out_specs = P("frame", "space", None, None, None)
    return jax.shard_map(
        per_device, mesh=mesh, in_specs=in_specs, out_specs=out_specs, check_vma=False
    )
```

```python
import jax
import jax.numpy as jnp
from jax import lax
from jax.experimental import pallas as pl
from jax.experimental.pallas import tpu as pltpu
from jax.sharding import PartitionSpec as P

MESH = pl.DeviceIdType.MESH
F32 = jnp.float32
BF16 = jnp.bfloat16
PAIRS = (1, 2, 0, 3)
INNER, OUTER = slice(0, 16), slice(16, 32)


def below(x, edge, row):
    return pltpu.roll(jnp.where(row == 7, edge, x), 1, axis=x.ndim - 2)


def above(x, edge, row):
    return pltpu.roll(jnp.where(row == 0, edge, x), 7, axis=x.ndim - 2)


def three(x, low, high, row):
    return below(x, low, row), x, above(x, high, row)


def pair(a, b):
    return jnp.concatenate([a, b], axis=-2).astype(BF16)


def put_layers(S, dy, at, rows, lanes, x):
    x = x.reshape((4, 2) + x.shape[1:])
    S[1, dy, at, 0:4, rows, lanes] = x[:, 0]
    S[0, dy, at, 1:5, rows, lanes] = x[:, 1]


def left_side(S, rows, start=0, count=4):
    pieces = []
    for zz in range(4):
        for dy in range(3):
            at = zz // 2 + start
            x = S[zz % 2, dy, :, at : at + count, rows, :]
            pieces.append(x.reshape(-1, 256))
    return jnp.concatenate(pieces, axis=1)


def kernel(
    feats, occ, wsp, bsp, wtm, fsend_h, fsrc_h, sahead_h, fprior_h, sback_h, flater_h, out,
    fsend, fsrc, sahead, fprior, sback, flater, fin, occv, wv, bv, wtv, M, H0, H1, ACC, S1, S2, SV, W0, W1, WT, VH, CR, msg, rmsg,
    sE, rE, sL, rL0, rL1, H2, BASE, lsem, msend, mrecv, esend, erecv, lsend, lrecv,
):
    s, f = lax.axis_index("space"), lax.axis_index("frame")
    n_s, n_f = lax.axis_size("space"), lax.axis_size("frame")
    lo, hi, be, af = s > 0, s < n_s - 1, f > 0, f < n_f - 1

    loads = [
        pltpu.make_async_copy(src, dst, lsem.at[i])
        for i, (src, dst) in enumerate(
            (
                (occ.at[0], occv), (feats.at[0], fin), (wsp, wv), (bsp, bv), (wtm, wtv),
                (fsend_h, fsend), (fsrc_h, fsrc), (sahead_h, sahead), (fprior_h, fprior),
                (sback_h, sback), (flater_h, flater),
            )
        )
    ]
    for c in loads:
        c.start()

    barrier = pltpu.get_barrier_semaphore()
    for there, to in (
        (lo, {"space": s - 1}),
        (hi, {"space": s + 1}),
        (be, {"frame": f - 1}),
        (af, {"frame": f + 1}),
    ):

        @pl.when(there)
        def _(to=to):
            pl.semaphore_signal(barrier, 1, device_id=to, device_id_type=MESH)

    lane = lax.broadcasted_iota(jnp.int32, (1, 1, 128), 2)
    left = lane < 64
    row = lax.broadcasted_iota(jnp.int32, (1, 8, 128), 1)
    row2 = lax.broadcasted_iota(jnp.int32, (8, 128), 0)

    loads[0].wait()
    voxel = lax.broadcasted_iota(jnp.int32, (64, 512), 1)
    mine = (voxel >> 3) == lax.broadcasted_iota(jnp.int32, (64, 512), 0)
    o = occv[...].astype(F32)
    spread = jnp.concatenate(
        [jnp.where(mine, o[b : b + 1, :], 0.0).astype(BF16) for b in range(4)], axis=0
    )
    r = lax.broadcasted_iota(jnp.int32, (16, 512), 0) & 7
    c = lax.broadcasted_iota(jnp.int32, (16, 512), 1) >> 6
    widen = jnp.where(r == c, 1.0, 0.0).astype(BF16)
    widen = jnp.concatenate([widen] * 32, axis=0)
    m = jnp.dot(spread, widen, preferred_element_type=F32)
    loads[1].wait()
    for g in range(4):
        mg = m[:, g * 128 : (g + 1) * 128].reshape(4, 4, 2, 8, 128)
        M[:, :, :, g] = mg
        x = fin[:, :, :, g * 128 : (g + 1) * 128].astype(F32)
        H0[:, :, :, g] = x.reshape(4, 4, 2, 8, 128) * mg

    for copy in loads[5:]:
        copy.wait()

    def tile(H, b, g):
        return H[b, :, :, g].reshape(8, 8, 128)

    def rim(b, face):
        e = fsrc[0, b, face]
        return e >= 2, jnp.maximum(e - 2, 0) // 6

    def rim_tile(H, b, face, g):
        has, j = rim(b, face)
        return jnp.where(has, tile(H, j, g), 0.0)

    def rim_layer(H, b, face, g):
        has, j = rim(b, face)
        z = 7 if face == 4 else 0
        return jnp.where(has, H[j, z // 2, z % 2, g], 0.0)

    down = jnp.maximum(fsend[0, 0], 0) // 6
    up = jnp.maximum(fsend[0, 1], 0) // 6

    def rows16(x):
        return x.reshape(-1, 128).astype(BF16).reshape(-1, 16, 128)

    def parcel(k, b, g, face, other):
        beyond = rim_tile(H0, b, face, other)
        mask = tile(M, b, g)
        asked = jnp.where(fsrc[0, b, face] == face, 1.0, 0.0)
        mixed = jnp.where(left, beyond, mask) if k == 0 else jnp.where(left, mask, beyond)
        edges = jnp.where(row == 0, rim_tile(H0, b, 3, g), asked)
        edges = jnp.where(row == 7, rim_tile(H0, b, 2, g), edges)
        msg[k, 0:4] = rows16(tile(H0, b, g))
        msg[k, 4:8] = rows16(mixed)
        msg[k, 8:12] = rows16(edges)
        msg[k, 12] = pair(rim_layer(H0, b, 4, g), rim_layer(H0, b, 5, g))

    parcel(0, up, 3, 1, 0)
    parcel(1, down, 0, 0, 3)

    for k, ends in ((0, s == 0), (1, s == n_s - 1)):

        @pl.when(ends)
        def _(k=k):
            rmsg[k] = jnp.zeros((13, 16, 128), BF16)

    loads[2].wait()
    loads[3].wait()
    nil = jnp.zeros((64, 64), BF16)
    nil_half = jnp.zeros((256, 128), BF16)

    W = (W0, W1)

    def band(layer):
        for yd in range(3):
            W[layer][yd * 256 : yd * 256 + 256, 128:256] = nil_half
            W[layer][(9 + yd) * 256 : (9 + yd) * 256 + 256, 0:128] = nil_half
        for zd in range(3):
            for yd in range(3):
                w0, w1, w2 = (wv[layer, 9 * zd + 3 * yd + k] for k in range(3))
                block = jnp.concatenate(
                    [
                        jnp.concatenate(ab, axis=1)
                        for ab in ((w1, w0), (w2, w1), (nil, w2), (w0, nil))
                    ],
                    axis=0,
                )
                at = (zd * 3 + yd) * 256
                W[layer][at : at + 256, 0:128] = block
                at = at + 768
                W[layer][at : at + 256, 128:256] = block

    band(0)

    here = lo.astype(jnp.int32) + hi.astype(jnp.int32) + be.astype(jnp.int32) + af.astype(jnp.int32)
    pl.semaphore_wait(barrier, here)

    def remote(src, dst, send, recv, to):
        return pltpu.make_async_remote_copy(
            src_ref=src, dst_ref=dst, send_sem=send, recv_sem=recv, device_id=to, device_id_type=MESH
        )

    upward = remote(msg.at[0], rmsg.at[0], msend.at[0], mrecv.at[0], {"space": s + 1})
    downward = remote(msg.at[1], rmsg.at[1], msend.at[1], mrecv.at[1], {"space": s - 1})

    @pl.when(hi)
    def _():
        upward.start()

    @pl.when(lo)
    def _():
        downward.start()

    def inner_rows(H, S, b):
        t = []
        for g in range(4):
            t.append(three(tile(H, b, g), rim_tile(H, b, 2, g), rim_tile(H, b, 3, g), row))
        for dy in range(3):
            put_layers(S, dy, b, INNER, slice(0, 128), pair(t[1][dy], t[2][dy]))
            e1 = jnp.where(left, t[2][dy], t[0][dy])
            e2 = jnp.where(left, t[3][dy], t[1][dy])
            put_layers(S, dy, b, INNER, slice(128, 256), pair(e1, e2))
        for face, at in ((4, (0, 0)), (5, (1, 4))):
            t = [three(rim_layer(H, b, face, g), 0.0, 0.0, row2) for g in range(4)]
            for dy in range(3):
                S[at[0], dy, b, at[1], INNER, 0:128] = pair(t[1][dy], t[2][dy])
                e1 = jnp.where(left[0], t[2][dy], t[0][dy])
                e2 = jnp.where(left[0], t[3][dy], t[1][dy])
                S[at[0], dy, b, at[1], INNER, 128:256] = pair(e1, e2)

    row16 = lax.broadcasted_iota(jnp.int32, (16, 128), 0)
    lane16 = lax.broadcasted_iota(jnp.int32, (16, 128), 1)
    near = (row16 < 8) == (lane16 < 64)

    def outer_rows(H, S, b, xl, xr):
        t = [
            three(tile(H, b, g), rim_tile(H, b, 2, g), rim_tile(H, b, 3, g), row) for g in (0, 3)
        ]
        xl = three(xl, 0.0, 0.0, row)
        xr = three(xr, 0.0, 0.0, row)
        for dy in range(3):
            put_layers(S, dy, b, OUTER, slice(0, 128), pair(t[0][dy], t[1][dy]))
            far = pair(xl[dy], xr[dy]).reshape(4, 2, 16, 128)
            for odd, at in ((0, slice(0, 4)), (1, slice(1, 5))):
                inner = S[1 - odd, dy, b, at, INNER, 0:128]
                S[1 - odd, dy, b, at, OUTER, 128:256] = jnp.where(near, inner, far[:, odd])
        for face, at in ((4, (0, 0)), (5, (1, 4))):
            t = [three(rim_layer(H, b, face, g), 0.0, 0.0, row2) for g in (0, 3)]
            for dy in range(3):
                S[at[0], dy, b, at[1], OUTER, 0:128] = pair(t[0][dy], t[1][dy])
                inner = S[at[0], dy, b, at[1], INNER, 0:128]
                S[at[0], dy, b, at[1], OUTER, 128:256] = jnp.where(near, inner, jnp.zeros((), BF16))

    @pl.loop(0, 4, unroll=True)
    def _(b):
        inner_rows(H0, S1, b)
        outer_rows(H0, S1, b, rim_tile(H0, b, 0, 3), rim_tile(H0, b, 1, 0))

    bias = [jnp.concatenate([bv[i : i + 1, :]] * 2, axis=1).reshape(1, 1, 1, 128) for i in range(2)]

    band(1)
    acc = jnp.dot(left_side(S1, slice(0, 32)), W0[...], preferred_element_type=F32)
    acc = acc.reshape(4, 4, 4, 8, 256)
    for i, g in enumerate(PAIRS):
        for oz in range(2):
            h = acc[:, :, i, :, oz * 128 : (oz + 1) * 128] + bias[0]
            if i >= 2:
                ACC[:, :, oz, i - 2] = h
            H1[:, :, oz, g] = jnp.maximum(h, 0.0) * M[:, :, oz, g]

    @pl.loop(0, 4, unroll=True)
    def _(b):
        inner_rows(H1, S2, b)

    def second(half, start, count):
        rows, layers = (INNER, OUTER)[half], slice(start, start + count)
        acc = jnp.dot(left_side(S2, rows, start, count), W1[...], preferred_element_type=F32)
        acc = acc.reshape(4, count, 2, 8, 256)
        for i in range(2):
            g = PAIRS[2 * half + i]
            h = [
                jnp.maximum(acc[:, :, i, :, oz * 128 : (oz + 1) * 128] + bias[1], 0.0)
                * M[:, layers, oz, g]
                for oz in range(2)
            ]
            H2[half, :, layers, :, i * 128 : (i + 1) * 128] = jnp.concatenate(h, axis=2).astype(BF16)

    def exchange(half, start, count, sent, got, sems):
        layers = slice(start, start + count)
        for k in range(3):
            sent[0, k] = H2[half, sahead[0, k], layers]
            sent[1, k] = H2[half, sback[0, k], layers]
        send, recv = sems
        ahead = remote(sent.at[0], got.at[0], send.at[0], recv.at[0], {"frame": f + 1})
        back = remote(sent.at[1], got.at[1], send.at[1], recv.at[1], {"frame": f - 1})

        @pl.when(af)
        def _():
            ahead.start()

        @pl.when(be)
        def _():
            back.start()

        return ahead, back

    second(0, 0, 4)
    early = exchange(0, 0, 4, sE, rE, (esend, erecv))

    for there, copy in ((lo, upward), (hi, downward)):

        @pl.when(there)
        def _(copy=copy):
            copy.wait_recv()

    def parts(k):
        x = rmsg[k].astype(F32)
        return (
            x[0:4].reshape(8, 8, 128),
            x[4:8].reshape(8, 8, 128),
            x[8:12].reshape(8, 8, 128),
            x[12].reshape(2, 8, 128),
        )

    got = [parts(0), parts(1)]
    own = (tile(H0, down, 0), tile(H0, up, 3))
    V = []
    for k in range(2):
        a, b, e, z = got[k]
        beyond = jnp.where(e[:, 3:4, :] > 0.5, own[k], b)
        V.append((three(a, e, e, row), three(beyond, 0.0, 0.0, row), three(z, 0.0, 0.0, row)))
    zero = jnp.zeros((8, 8, 128), F32)
    thin = jnp.zeros((16, 128), BF16)
    for dy in range(3):
        put_layers(SV, dy, 0, INNER, slice(0, 128), pair(V[0][0][dy], V[1][0][dy]))
        put_layers(SV, dy, 0, INNER, slice(128, 256), pair(V[0][1][dy], V[1][1][dy]))
        put_layers(SV, dy, 0, OUTER, slice(0, 128), pair(zero, zero))
        x0 = jnp.where(left, 0.0, three(got[0][0], 0.0, 0.0, row)[dy])
        x1 = jnp.where(left, three(got[1][0], 0.0, 0.0, row)[dy], 0.0)
        put_layers(SV, dy, 0, OUTER, slice(128, 256), pair(x0, x1))
        for z, at in ((0, (0, 0)), (1, (1, 4))):
            SV[at[0], dy, 0, at[1], INNER, 0:128] = pair(V[0][2][dy][z], V[1][2][dy][z])
            SV[at[0], dy, 0, at[1], INNER, 128:256] = thin
            SV[at[0], dy, 0, at[1], OUTER, 0:128] = thin
            SV[at[0], dy, 0, at[1], OUTER, 128:256] = thin

    acc = jnp.dot(left_side(SV, slice(0, 32)), W0[...], preferred_element_type=F32)
    acc = acc.reshape(4, 4, 8, 256)
    for k in range(2):
        for oz in range(2):
            lanes = slice(oz * 128, (oz + 1) * 128)
            mask = got[k][1].reshape(4, 2, 8, 128)[:, oz]
            VH[k, :, oz] = jnp.maximum(acc[:, k, :, lanes] + bias[0][0], 0.0) * mask
            CR[k, :, oz] = acc[:, 2 + k, :, lanes]

    @pl.loop(0, 4, unroll=True)
    def _(b):
        for k, g in ((0, 0), (1, 3)):
            h = ACC[b, :, :, k] + jnp.where(fsrc[0, b, k] == k, CR[k], 0.0)
            H1[b, :, :, g] = jnp.maximum(h, 0.0) * M[b, :, :, g]

    @pl.loop(0, 4, unroll=True)
    def _(b):
        x = []
        for k, g in ((0, 3), (1, 0)):
            far = VH[k].reshape(8, 8, 128)
            x.append(jnp.where(fsrc[0, b, k] == k, far, rim_tile(H1, b, k, g)))
        outer_rows(H1, S2, b, x[0], x[1])

    late = []
    rL = (rL0, rL1)
    for n in range(2):
        second(1, 2 * n, 2)
        late.append(exchange(1, 2 * n, 2, sL.at[n], rL[n], (lsend.at[n], lrecv.at[n])))
    loads[4].wait()
    for k in range(3):
        w = wtv[k]
        two = jnp.concatenate(
            [jnp.concatenate([w, nil], axis=1), jnp.concatenate([nil, w], axis=1)], axis=0
        )
        WT[k, 0:128, 0:128] = two
        WT[k, 128:256, 128:256] = two
        WT[k, 0:128, 128:256] = jnp.zeros((128, 128), BF16)
        WT[k, 128:256, 0:128] = jnp.zeros((128, 128), BF16)

    def wide(H, g):
        return H[:, :, :, g].reshape(4, 4, 16, 128)

    def base(half):
        t = jnp.dot(H2[half].reshape(256, 256), WT[1], preferred_element_type=F32)
        t = t.reshape(4, 4, 16, 256)
        for i in range(2):
            g = PAIRS[2 * half + i]
            lanes = slice(i * 128, (i + 1) * 128)
            BASE[half, :, :, :, lanes] = t[:, :, :, lanes] + wide(H0, g)


    base(0)
    base(1)

    def finish(half, start, count, copies, got):
        ahead, back = copies
        layers = slice(start, start + count)

        @pl.when(be)
        def _():
            ahead.wait_recv()

        @pl.when(af)
        def _():
            back.wait_recv()

        lhs = []
        for b in range(4):
            p, q = fprior[0, b], flater[0, b]
            x = jnp.where(p >= 0, got[0, jnp.maximum(p, 0)].astype(F32), 0.0).astype(BF16)
            y = jnp.where(q >= 0, got[1, jnp.maximum(q, 0)].astype(F32), 0.0).astype(BF16)
            lhs.append(jnp.concatenate([x.reshape(-1, 256), y.reshape(-1, 256)], axis=1))
        wt = jnp.concatenate([WT[0], WT[2]], axis=0)
        t = jnp.dot(jnp.concatenate(lhs, axis=0), wt, preferred_element_type=F32)
        t = t.reshape(4, count, 16, 256)
        for i in range(2):
            g = PAIRS[2 * half + i]
            lanes = slice(i * 128, (i + 1) * 128)
            mask = M[:, layers, :, g].reshape(4, count, 16, 128)
            x = (BASE[half, :, layers, :, lanes] + t[:, :, :, lanes]) * mask
            x = x.reshape(4, 2 * count, 8, 128).astype(BF16)
            out[0, :, 2 * start : 2 * (start + count), :, g * 128 : (g + 1) * 128] = x

    finish(0, 0, 4, early, rE)
    for n in range(2):
        finish(1, 2 * n, 2, late[n], rL[n])

    for there, copies in (
        (hi, (upward,)),
        (lo, (downward,)),
        (af, (early[0], late[0][0], late[1][0])),
        (be, (early[1], late[0][1], late[1][1])),
    ):

        @pl.when(there)
        def _(copies=copies):
            for c in copies:
                c.wait_send()


def per_device(*args):
    field = (4, 4, 2, 4, 8, 128)
    hbm = pl.BlockSpec(memory_space=pltpu.HBM)
    left = (2, 3, 4, 5, 32, 256)
    parcels = (2, 3, 4, 16, 256)
    halves = (2, 2, 3, 2, 16, 256)
    return pl.pallas_call(
        kernel,
        out_shape=pltpu.VMEM((1, 4, 8, 8, 512), BF16),
        in_specs=[hbm] * 11,
        out_specs=pl.BlockSpec(memory_space=pltpu.VMEM),
        scratch_shapes=[
            pltpu.SMEM((1, 2), jnp.int32),
            pltpu.SMEM((1, 4, 6), jnp.int32),
            pltpu.SMEM((1, 3), jnp.int32),
            pltpu.SMEM((1, 4), jnp.int32),
            pltpu.SMEM((1, 3), jnp.int32),
            pltpu.SMEM((1, 4), jnp.int32),
            pltpu.VMEM((4, 8, 8, 512), BF16),
            pltpu.VMEM((4, 512), jnp.int32),
            pltpu.VMEM((2, 27, 64, 64), BF16),
            pltpu.VMEM((2, 64), F32),
            pltpu.VMEM((3, 64, 64), BF16),
            pltpu.VMEM(field, F32),
            pltpu.VMEM(field, F32),
            pltpu.VMEM(field, F32),
            pltpu.VMEM((4, 4, 2, 2, 8, 128), F32),
            pltpu.VMEM(left, BF16),
            pltpu.VMEM(left, BF16),
            pltpu.VMEM((2, 3, 1, 5, 32, 256), BF16),
            pltpu.VMEM((3072, 256), BF16),
            pltpu.VMEM((3072, 256), BF16),
            pltpu.VMEM((3, 256, 256), BF16),
            pltpu.VMEM((2, 4, 2, 8, 128), F32),
            pltpu.VMEM((2, 4, 2, 8, 128), F32),
            pltpu.VMEM((2, 13, 16, 128), BF16),
            pltpu.VMEM((2, 13, 16, 128), BF16),
            pltpu.VMEM(parcels, BF16),
            pltpu.VMEM(parcels, BF16),
            pltpu.VMEM(halves, BF16),
            pltpu.VMEM(halves[1:], BF16),
            pltpu.VMEM(halves[1:], BF16),
            pltpu.VMEM((2, 4, 4, 16, 256), BF16),
            pltpu.VMEM((2, 4, 4, 16, 256), F32),
            pltpu.SemaphoreType.DMA((11,)),
        ]
        + [pltpu.SemaphoreType.DMA((2,))] * 4
        + [pltpu.SemaphoreType.DMA((2, 2))] * 2,
        compiler_params=pltpu.CompilerParams(
            collective_id=0, has_side_effects=True, vmem_limit_bytes=56 << 20
        ),
    )(*args)


def solution(mesh):
    in_specs = (
        P("frame", "space", None, None, None),
        P("frame", "space", None),
        P(),
        P(),
        P(),
        P("frame", "space"),
        P("frame", "space", None),
        P("frame", "space"),
        P("frame", "space"),
        P("frame", "space"),
        P("frame", "space"),
    )
    out_specs = P("frame", "space", None, None, None)
    return jax.shard_map(
        per_device, mesh=mesh, in_specs=in_specs, out_specs=out_specs, check_vma=False
    )
```

```python
import jax
import jax.numpy as jnp
from jax import lax
from jax.experimental import pallas as pl
from jax.experimental.pallas import tpu as pltpu
from jax.sharding import PartitionSpec as P

MESH = pl.DeviceIdType.MESH
F32 = jnp.float32
BF16 = jnp.bfloat16
PAIRS = (1, 2, 0, 3)
INNER, OUTER = slice(0, 16), slice(16, 32)


def below(x, edge, row):
    return pltpu.roll(jnp.where(row == 7, edge, x), 1, axis=x.ndim - 2)


def above(x, edge, row):
    return pltpu.roll(jnp.where(row == 0, edge, x), 7, axis=x.ndim - 2)


def three(x, low, high, row):
    return below(x, low, row), x, above(x, high, row)


def pair(a, b):
    return jnp.concatenate([a, b], axis=-2).astype(BF16)


def put_layers(S, dy, at, rows, lanes, x):
    x = x.reshape((4, 2) + x.shape[1:])
    S[1, dy, at, 0:4, rows, lanes] = x[:, 0]
    S[0, dy, at, 1:5, rows, lanes] = x[:, 1]


def left_side(S, rows, start=0, count=4):
    pieces = []
    for zz in range(4):
        for dy in range(3):
            at = zz // 2 + start
            x = S[zz % 2, dy, :, at : at + count, rows, :]
            pieces.append(x.reshape(-1, 256))
    return jnp.concatenate(pieces, axis=1)


def kernel(
    feats, occ, wsp, bsp, wtm, fsend_h, fsrc_h, sahead_h, fprior_h, sback_h, flater_h, out,
    fsend, fsrc, sahead, fprior, sback, flater, fin, occv, wv, bv, wtv, M, H0, H1, ACC, S1, S2, SV, W0, W1, WT, VH, CR, msg, rmsg,
    sE, rE, sL, rL0, rL1, H2, BASE, lsem, msend, mrecv, esend, erecv, lsend, lrecv,
):
    s, f = lax.axis_index("space"), lax.axis_index("frame")
    n_s, n_f = lax.axis_size("space"), lax.axis_size("frame")
    lo, hi, be, af = s > 0, s < n_s - 1, f > 0, f < n_f - 1

    loads = [
        pltpu.make_async_copy(src, dst, lsem.at[i])
        for i, (src, dst) in enumerate(
            (
                (occ.at[0], occv), (feats.at[0], fin), (wsp, wv), (bsp, bv), (wtm, wtv),
                (fsend_h, fsend), (fsrc_h, fsrc), (sahead_h, sahead), (fprior_h, fprior),
                (sback_h, sback), (flater_h, flater),
            )
        )
    ]
    for c in loads:
        c.start()

    barrier = pltpu.get_barrier_semaphore()
    for there, to in (
        (lo, {"space": s - 1}),
        (hi, {"space": s + 1}),
        (be, {"frame": f - 1}),
        (af, {"frame": f + 1}),
    ):

        @pl.when(there)
        def _(to=to):
            pl.semaphore_signal(barrier, 1, device_id=to, device_id_type=MESH)

    lane = lax.broadcasted_iota(jnp.int32, (1, 1, 128), 2)
    left = lane < 64
    row = lax.broadcasted_iota(jnp.int32, (1, 8, 128), 1)
    row2 = lax.broadcasted_iota(jnp.int32, (8, 128), 0)

    loads[0].wait()
    voxel = lax.broadcasted_iota(jnp.int32, (64, 512), 1)
    mine = (voxel >> 3) == lax.broadcasted_iota(jnp.int32, (64, 512), 0)
    o = occv[...].astype(F32)
    spread = jnp.concatenate(
        [jnp.where(mine, o[b : b + 1, :], 0.0).astype(BF16) for b in range(4)], axis=0
    )
    r = lax.broadcasted_iota(jnp.int32, (16, 512), 0) & 7
    c = lax.broadcasted_iota(jnp.int32, (16, 512), 1) >> 6
    widen = jnp.where(r == c, 1.0, 0.0).astype(BF16)
    widen = jnp.concatenate([widen] * 32, axis=0)
    m = jnp.dot(spread, widen, preferred_element_type=F32)
    loads[1].wait()
    for g in range(4):
        mg = m[:, g * 128 : (g + 1) * 128].reshape(4, 4, 2, 8, 128)
        M[:, :, :, g] = mg
        x = fin[:, :, :, g * 128 : (g + 1) * 128].astype(F32)
        H0[:, :, :, g] = x.reshape(4, 4, 2, 8, 128) * mg

    for copy in loads[5:]:
        copy.wait()

    def tile(H, b, g):
        return H[b, :, :, g].reshape(8, 8, 128)

    def rim(b, face):
        e = fsrc[0, b, face]
        return e >= 2, jnp.maximum(e - 2, 0) // 6

    def rim_tile(H, b, face, g):
        has, j = rim(b, face)
        return jnp.where(has, tile(H, j, g), 0.0)

    def rim_layer(H, b, face, g):
        has, j = rim(b, face)
        z = 7 if face == 4 else 0
        return jnp.where(has, H[j, z // 2, z % 2, g], 0.0)

    down = jnp.maximum(fsend[0, 0], 0) // 6
    up = jnp.maximum(fsend[0, 1], 0) // 6

    def rows16(x):
        return x.reshape(-1, 128).astype(BF16).reshape(-1, 16, 128)

    def parcel(k, b, g, face, other):
        beyond = rim_tile(H0, b, face, other)
        mask = tile(M, b, g)
        asked = jnp.where(fsrc[0, b, face] == face, 1.0, 0.0)
        mixed = jnp.where(left, beyond, mask) if k == 0 else jnp.where(left, mask, beyond)
        edges = jnp.where(row == 0, rim_tile(H0, b, 3, g), asked)
        edges = jnp.where(row == 7, rim_tile(H0, b, 2, g), edges)
        msg[k, 0:4] = rows16(tile(H0, b, g))
        msg[k, 4:8] = rows16(mixed)
        msg[k, 8:12] = rows16(edges)
        msg[k, 12] = pair(rim_layer(H0, b, 4, g), rim_layer(H0, b, 5, g))

    parcel(0, up, 3, 1, 0)
    parcel(1, down, 0, 0, 3)

    for k, ends in ((0, s == 0), (1, s == n_s - 1)):

        @pl.when(ends)
        def _(k=k):
            rmsg[k] = jnp.zeros((13, 16, 128), BF16)

    loads[2].wait()
    loads[3].wait()
    nil = jnp.zeros((64, 64), BF16)
    nil_half = jnp.zeros((256, 128), BF16)

    W = (W0, W1)

    def band(layer):
        for yd in range(3):
            W[layer][yd * 256 : yd * 256 + 256, 128:256] = nil_half
            W[layer][(9 + yd) * 256 : (9 + yd) * 256 + 256, 0:128] = nil_half
        for zd in range(3):
            for yd in range(3):
                w0, w1, w2 = (wv[layer, 9 * zd + 3 * yd + k] for k in range(3))
                block = jnp.concatenate(
                    [
                        jnp.concatenate(ab, axis=1)
                        for ab in ((w1, w0), (w2, w1), (nil, w2), (w0, nil))
                    ],
                    axis=0,
                )
                at = (zd * 3 + yd) * 256
                W[layer][at : at + 256, 0:128] = block
                at = at + 768
                W[layer][at : at + 256, 128:256] = block

    band(0)

    here = lo.astype(jnp.int32) + hi.astype(jnp.int32) + be.astype(jnp.int32) + af.astype(jnp.int32)
    pl.semaphore_wait(barrier, here)

    def remote(src, dst, send, recv, to):
        return pltpu.make_async_remote_copy(
            src_ref=src, dst_ref=dst, send_sem=send, recv_sem=recv, device_id=to, device_id_type=MESH
        )

    upward = remote(msg.at[0], rmsg.at[0], msend.at[0], mrecv.at[0], {"space": s + 1})
    downward = remote(msg.at[1], rmsg.at[1], msend.at[1], mrecv.at[1], {"space": s - 1})

    @pl.when(hi)
    def _():
        upward.start()

    @pl.when(lo)
    def _():
        downward.start()

    def inner_rows(H, S, b):
        t = []
        for g in range(4):
            t.append(three(tile(H, b, g), rim_tile(H, b, 2, g), rim_tile(H, b, 3, g), row))
        for dy in range(3):
            put_layers(S, dy, b, INNER, slice(0, 128), pair(t[1][dy], t[2][dy]))
            e1 = jnp.where(left, t[2][dy], t[0][dy])
            e2 = jnp.where(left, t[3][dy], t[1][dy])
            put_layers(S, dy, b, INNER, slice(128, 256), pair(e1, e2))
        for face, at in ((4, (0, 0)), (5, (1, 4))):
            t = [three(rim_layer(H, b, face, g), 0.0, 0.0, row2) for g in range(4)]
            for dy in range(3):
                S[at[0], dy, b, at[1], INNER, 0:128] = pair(t[1][dy], t[2][dy])
                e1 = jnp.where(left[0], t[2][dy], t[0][dy])
                e2 = jnp.where(left[0], t[3][dy], t[1][dy])
                S[at[0], dy, b, at[1], INNER, 128:256] = pair(e1, e2)

    row16 = lax.broadcasted_iota(jnp.int32, (16, 128), 0)
    lane16 = lax.broadcasted_iota(jnp.int32, (16, 128), 1)
    near = (row16 < 8) == (lane16 < 64)

    def outer_rows(H, S, b, xl, xr):
        t = [
            three(tile(H, b, g), rim_tile(H, b, 2, g), rim_tile(H, b, 3, g), row) for g in (0, 3)
        ]
        xl = three(xl, 0.0, 0.0, row)
        xr = three(xr, 0.0, 0.0, row)
        for dy in range(3):
            put_layers(S, dy, b, OUTER, slice(0, 128), pair(t[0][dy], t[1][dy]))
            far = pair(xl[dy], xr[dy]).reshape(4, 2, 16, 128)
            for odd, at in ((0, slice(0, 4)), (1, slice(1, 5))):
                inner = S[1 - odd, dy, b, at, INNER, 0:128]
                S[1 - odd, dy, b, at, OUTER, 128:256] = jnp.where(near, inner, far[:, odd])
        for face, at in ((4, (0, 0)), (5, (1, 4))):
            t = [three(rim_layer(H, b, face, g), 0.0, 0.0, row2) for g in (0, 3)]
            for dy in range(3):
                S[at[0], dy, b, at[1], OUTER, 0:128] = pair(t[0][dy], t[1][dy])
                inner = S[at[0], dy, b, at[1], INNER, 0:128]
                S[at[0], dy, b, at[1], OUTER, 128:256] = jnp.where(near, inner, jnp.zeros((), BF16))

    @pl.loop(0, 4, unroll=True)
    def _(b):
        inner_rows(H0, S1, b)
        outer_rows(H0, S1, b, rim_tile(H0, b, 0, 3), rim_tile(H0, b, 1, 0))

    bias = [jnp.concatenate([bv[i : i + 1, :]] * 2, axis=1).reshape(1, 1, 1, 128) for i in range(2)]

    band(1)
    acc = jnp.dot(left_side(S1, slice(0, 32)), W0[...], preferred_element_type=F32)
    acc = acc.reshape(4, 4, 4, 8, 256)
    for i, g in enumerate(PAIRS):
        for oz in range(2):
            h = acc[:, :, i, :, oz * 128 : (oz + 1) * 128] + bias[0]
            if i >= 2:
                ACC[:, :, oz, i - 2] = h
            H1[:, :, oz, g] = jnp.maximum(h, 0.0) * M[:, :, oz, g]

    @pl.loop(0, 4, unroll=True)
    def _(b):
        inner_rows(H1, S2, b)

    def second(half, start, count):
        rows, layers = (INNER, OUTER)[half], slice(start, start + count)
        acc = jnp.dot(left_side(S2, rows, start, count), W1[...], preferred_element_type=F32)
        acc = acc.reshape(4, count, 2, 8, 256)
        for i in range(2):
            g = PAIRS[2 * half + i]
            h = [
                jnp.maximum(acc[:, :, i, :, oz * 128 : (oz + 1) * 128] + bias[1], 0.0)
                * M[:, layers, oz, g]
                for oz in range(2)
            ]
            H2[half, :, layers, :, i * 128 : (i + 1) * 128] = jnp.concatenate(h, axis=2).astype(BF16)

    def exchange(half, start, count, sent, got, sems):
        layers = slice(start, start + count)
        for k in range(3):
            sent[0, k] = H2[half, sahead[0, k], layers]
            sent[1, k] = H2[half, sback[0, k], layers]
        send, recv = sems
        ahead = remote(sent.at[0], got.at[0], send.at[0], recv.at[0], {"frame": f + 1})
        back = remote(sent.at[1], got.at[1], send.at[1], recv.at[1], {"frame": f - 1})

        @pl.when(af)
        def _():
            ahead.start()

        @pl.when(be)
        def _():
            back.start()

        return ahead, back

    second(0, 0, 4)
    early = exchange(0, 0, 4, sE, rE, (esend, erecv))

    for there, copy in ((lo, upward), (hi, downward)):

        @pl.when(there)
        def _(copy=copy):
            copy.wait_recv()

    def parts(k):
        x = rmsg[k].astype(F32)
        return (
            x[0:4].reshape(8, 8, 128),
            x[4:8].reshape(8, 8, 128),
            x[8:12].reshape(8, 8, 128),
            x[12].reshape(2, 8, 128),
        )

    got = [parts(0), parts(1)]
    own = (tile(H0, down, 0), tile(H0, up, 3))
    V = []
    for k in range(2):
        a, b, e, z = got[k]
        beyond = jnp.where(e[:, 3:4, :] > 0.5, own[k], b)
        V.append((three(a, e, e, row), three(beyond, 0.0, 0.0, row), three(z, 0.0, 0.0, row)))
    zero = jnp.zeros((8, 8, 128), F32)
    plain = [three(got[k][0], 0.0, 0.0, row) for k in range(2)]
    thin = jnp.zeros((16, 128), BF16)
    for dy in range(3):
        put_layers(SV, dy, 0, INNER, slice(0, 128), pair(V[0][0][dy], V[1][0][dy]))
        put_layers(SV, dy, 0, INNER, slice(128, 256), pair(V[0][1][dy], V[1][1][dy]))
        put_layers(SV, dy, 0, OUTER, slice(0, 128), pair(zero, zero))
        x0 = jnp.where(left, 0.0, plain[0][dy])
        x1 = jnp.where(left, plain[1][dy], 0.0)
        put_layers(SV, dy, 0, OUTER, slice(128, 256), pair(x0, x1))
        for z, at in ((0, (0, 0)), (1, (1, 4))):
            SV[at[0], dy, 0, at[1], INNER, 0:128] = pair(V[0][2][dy][z], V[1][2][dy][z])
            SV[at[0], dy, 0, at[1], INNER, 128:256] = thin
            SV[at[0], dy, 0, at[1], OUTER, 0:128] = thin
            SV[at[0], dy, 0, at[1], OUTER, 128:256] = thin

    acc = jnp.dot(left_side(SV, slice(0, 32)), W0[...], preferred_element_type=F32)
    acc = acc.reshape(4, 4, 8, 256)
    for k in range(2):
        for oz in range(2):
            lanes = slice(oz * 128, (oz + 1) * 128)
            mask = got[k][1].reshape(4, 2, 8, 128)[:, oz]
            VH[k, :, oz] = jnp.maximum(acc[:, k, :, lanes] + bias[0][0], 0.0) * mask
            CR[k, :, oz] = acc[:, 2 + k, :, lanes]

    @pl.loop(0, 4, unroll=True)
    def _(b):
        for k, g in ((0, 0), (1, 3)):
            h = ACC[b, :, :, k] + jnp.where(fsrc[0, b, k] == k, CR[k], 0.0)
            H1[b, :, :, g] = jnp.maximum(h, 0.0) * M[b, :, :, g]

    @pl.loop(0, 4, unroll=True)
    def _(b):
        x = []
        for k, g in ((0, 3), (1, 0)):
            far = VH[k].reshape(8, 8, 128)
            x.append(jnp.where(fsrc[0, b, k] == k, far, rim_tile(H1, b, k, g)))
        outer_rows(H1, S2, b, x[0], x[1])

    late = []
    rL = (rL0, rL1)
    for n in range(2):
        second(1, 2 * n, 2)
        late.append(exchange(1, 2 * n, 2, sL.at[n], rL[n], (lsend.at[n], lrecv.at[n])))
    loads[4].wait()
    for k in range(3):
        w = wtv[k]
        two = jnp.concatenate(
            [jnp.concatenate([w, nil], axis=1), jnp.concatenate([nil, w], axis=1)], axis=0
        )
        WT[k, 0:128, 0:128] = two
        WT[k, 128:256, 128:256] = two
        WT[k, 0:128, 128:256] = jnp.zeros((128, 128), BF16)
        WT[k, 128:256, 0:128] = jnp.zeros((128, 128), BF16)

    def wide(H, g):
        return H[:, :, :, g].reshape(4, 4, 16, 128)

    def base(half):
        t = jnp.dot(H2[half].reshape(256, 256), WT[1], preferred_element_type=F32)
        t = t.reshape(4, 4, 16, 256)
        for i in range(2):
            g = PAIRS[2 * half + i]
            lanes = slice(i * 128, (i + 1) * 128)
            BASE[half, :, :, :, lanes] = t[:, :, :, lanes] + wide(H0, g)


    base(0)
    base(1)

    def finish(half, start, count, copies, got):
        ahead, back = copies
        layers = slice(start, start + count)

        @pl.when(be)
        def _():
            ahead.wait_recv()

        @pl.when(af)
        def _():
            back.wait_recv()

        lhs = []
        for b in range(4):
            p, q = fprior[0, b], flater[0, b]
            x = jnp.where(p >= 0, got[0, jnp.maximum(p, 0)], jnp.zeros((), BF16))
            y = jnp.where(q >= 0, got[1, jnp.maximum(q, 0)], jnp.zeros((), BF16))
            lhs.append(jnp.concatenate([x.reshape(-1, 256), y.reshape(-1, 256)], axis=1))
        wt = jnp.concatenate([WT[0], WT[2]], axis=0)
        t = jnp.dot(jnp.concatenate(lhs, axis=0), wt, preferred_element_type=F32)
        t = t.reshape(4, count, 16, 256)
        for i in range(2):
            g = PAIRS[2 * half + i]
            lanes = slice(i * 128, (i + 1) * 128)
            mask = M[:, layers, :, g].reshape(4, count, 16, 128)
            x = (BASE[half, :, layers, :, lanes] + t[:, :, :, lanes]) * mask
            x = x.reshape(4, 2 * count, 8, 128).astype(BF16)
            out[0, :, 2 * start : 2 * (start + count), :, g * 128 : (g + 1) * 128] = x

    finish(0, 0, 4, early, rE)
    for n in range(2):
        finish(1, 2 * n, 2, late[n], rL[n])

    for there, copies in (
        (hi, (upward,)),
        (lo, (downward,)),
        (af, (early[0], late[0][0], late[1][0])),
        (be, (early[1], late[0][1], late[1][1])),
    ):

        @pl.when(there)
        def _(copies=copies):
            for c in copies:
                c.wait_send()


def per_device(*args):
    field = (4, 4, 2, 4, 8, 128)
    hbm = pl.BlockSpec(memory_space=pltpu.HBM)
    left = (2, 3, 4, 5, 32, 256)
    parcels = (2, 3, 4, 16, 256)
    halves = (2, 2, 3, 2, 16, 256)
    return pl.pallas_call(
        kernel,
        out_shape=pltpu.VMEM((1, 4, 8, 8, 512), BF16),
        in_specs=[hbm] * 11,
        out_specs=pl.BlockSpec(memory_space=pltpu.VMEM),
        scratch_shapes=[
            pltpu.SMEM((1, 2), jnp.int32),
            pltpu.SMEM((1, 4, 6), jnp.int32),
            pltpu.SMEM((1, 3), jnp.int32),
            pltpu.SMEM((1, 4), jnp.int32),
            pltpu.SMEM((1, 3), jnp.int32),
            pltpu.SMEM((1, 4), jnp.int32),
            pltpu.VMEM((4, 8, 8, 512), BF16),
            pltpu.VMEM((4, 512), jnp.int32),
            pltpu.VMEM((2, 27, 64, 64), BF16),
            pltpu.VMEM((2, 64), F32),
            pltpu.VMEM((3, 64, 64), BF16),
            pltpu.VMEM(field, F32),
            pltpu.VMEM(field, F32),
            pltpu.VMEM(field, F32),
            pltpu.VMEM((4, 4, 2, 2, 8, 128), F32),
            pltpu.VMEM(left, BF16),
            pltpu.VMEM(left, BF16),
            pltpu.VMEM((2, 3, 1, 5, 32, 256), BF16),
            pltpu.VMEM((3072, 256), BF16),
            pltpu.VMEM((3072, 256), BF16),
            pltpu.VMEM((3, 256, 256), BF16),
            pltpu.VMEM((2, 4, 2, 8, 128), F32),
            pltpu.VMEM((2, 4, 2, 8, 128), F32),
            pltpu.VMEM((2, 13, 16, 128), BF16),
            pltpu.VMEM((2, 13, 16, 128), BF16),
            pltpu.VMEM(parcels, BF16),
            pltpu.VMEM(parcels, BF16),
            pltpu.VMEM(halves, BF16),
            pltpu.VMEM(halves[1:], BF16),
            pltpu.VMEM(halves[1:], BF16),
            pltpu.VMEM((2, 4, 4, 16, 256), BF16),
            pltpu.VMEM((2, 4, 4, 16, 256), F32),
            pltpu.SemaphoreType.DMA((11,)),
        ]
        + [pltpu.SemaphoreType.DMA((2,))] * 4
        + [pltpu.SemaphoreType.DMA((2, 2))] * 2,
        compiler_params=pltpu.CompilerParams(
            collective_id=0, has_side_effects=True, vmem_limit_bytes=56 << 20
        ),
    )(*args)


def solution(mesh):
    in_specs = (
        P("frame", "space", None, None, None),
        P("frame", "space", None),
        P(),
        P(),
        P(),
        P("frame", "space"),
        P("frame", "space", None),
        P("frame", "space"),
        P("frame", "space"),
        P("frame", "space"),
        P("frame", "space"),
    )
    out_specs = P("frame", "space", None, None, None)
    return jax.shard_map(
        per_device, mesh=mesh, in_specs=in_specs, out_specs=out_specs, check_vma=False
    )
```
